256 devices in a mesh: prow: 8 (over x, core), pcol: 32 (over z, y).
Axes of the slice: x: 4, y: 4, z: 8, core: 2. Of those that a mesh axis runs over, the one named last changes fastest.
Arguments:
- panel_rhs: float32 [512, 2, 1024], P('prow', None, 'pcol'), may hold values from -6 to 6
- diag_inv: float32 [2, 1024, 1024], P(None, 'pcol'), may hold values from -1 to 2, as said below
- coupling: float32 [1024, 1024], P('pcol'), may hold values from -0.1875 to 0.1875
- trail_factor: float32 [2, 1024, 114688], P(None, 'pcol', 'prow'), may hold values from -0.125 to 0.125
- trail_rhs: float32 [512, 114688], P('pcol', 'prow'), may hold values from -6 to 6
Outputs:
- solved: float32 [512, 2, 1024], P('prow', None, 'pcol')
- trail_reduced: float32 [512, 114688], P('pcol', 'prow')
The draws below stay inside these ranges and needn't reach their ends.
Inputs may be any that keep to these rules, and one draw needn't show every extreme that they name: Each diag_inv[k] is upper triangular, with diagonal entries between 0.4 and 2.
All inputs are finite; a program needn't handle non-finite values.
Results may differ from the reference program's by a relative error of at most 0.000096.
Values sent between devices are 32-bit elements; how exact they have to be, the bound alone decides.
No kernel may reach another device: no remote copies, remote signals or barrier semaphores. Data moves between devices by JAX's collectives and lax.ppermute only.
A program may use at most 128 MiB of HBM per device.

```python
import jax
import jax.numpy as jnp
from jax import lax

NB = 1024
NRHS = 512
M = 114688


def draw_diag_inv(key, part):
    key = jax.random.fold_in(key, 7)
    key_diag, key_off = jax.random.split(key)
    diag_vals = jax.random.uniform(key_diag, (2, NB), jnp.float32, 0.6, 1.6)
    off_vals = jax.random.truncated_normal(key_off, -3.0, 3.0, (2, NB, NB), jnp.float32) * (0.5 / NB ** 0.5)
    row_ids = jax.lax.broadcasted_iota(jnp.int32, (2, NB, NB), 1)
    col_ids = jax.lax.broadcasted_iota(jnp.int32, (2, NB, NB), 2)
    upper = jnp.where(row_ids < col_ids, off_vals, 0.0)
    return upper + jnp.where(row_ids == col_ids, diag_vals[:, :, None], 0.0)


def shard_levels(rng, extent, shards, low, top_value):
    def one(dim, parts):
        heights = jax.random.uniform(jax.random.fold_in(jax.random.fold_in(rng, 6), dim), (parts,), jnp.float32, low / len(shards), top_value / len(shards))
        return jnp.repeat(jnp.exp(heights), extent[dim] // parts).reshape((-1,) + (1,) * (len(extent) - dim - 1))

    level = one(*shards[0])
    for cut in shards[1:]:
        level = level * one(*cut)
    return level


def bell_draw(own_key, dims, deviation, bound, shards=(), kind=jnp.bfloat16):
    values = jax.random.normal(own_key, dims, jnp.float32) * deviation
    if len(shards) > 0:
        values = shard_levels(own_key, dims, shards, -0.22, 0.18) * values
    return jnp.clip(values, min=-bound, max=bound).astype(kind)


def setup_inputs(seed: int = 0) -> dict:
    key_of = jax.random.split(jax.random.key(seed), 6)
    return {
        "panel_rhs": bell_draw(key_of[0], (NRHS, 2, NB), 1.0, 6.0, ((0, 8), (2, 32)), jnp.float32),
        "diag_inv": draw_diag_inv(jax.random.fold_in(key_of[5], 71), 0),
        "coupling": bell_draw(key_of[2], (NB, NB), NB ** -0.5, 0.1875, ((0, 32),), jnp.float32),
        "trail_factor": bell_draw(key_of[3], (2, NB, M), (2 * NB) ** -0.5, 0.125, ((1, 32), (2, 8)), jnp.float32),
        "trail_rhs": bell_draw(key_of[4], (NRHS, M), 1.0, 6.0, ((0, 32), (1, 8)), jnp.float32),
    }


def product(left, right):
    return jnp.dot(left, right, preferred_element_type=jnp.float32, precision=lax.Precision.HIGHEST)


def reference(panel_rhs, diag_inv, coupling, trail_factor, trail_rhs):
    first = product(panel_rhs[:, 0, :], diag_inv[0])
    second = panel_rhs[:, 1, :] - product(first, coupling)
    latter = product(second, diag_inv[1])
    solved = jnp.stack([first, latter], axis=1)
    update = product(first, trail_factor[0]) + product(latter, trail_factor[1])
    return solved, trail_rhs - update
```

```python
import jax
import jax.numpy as jnp
from jax import lax
from jax.sharding import Mesh, PartitionSpec as P

X, C, Z, Y = 4, 2, 8, 4
ROWS = ("x", "c")
COLS = ("z", "y")
SPREAD = ("x", "c", "y")
QUAD = 4


def einsum(form, left, right, precision=lax.Precision.HIGHEST):
    return jnp.einsum(form, left, right, preferred_element_type=jnp.float32, precision=precision)


def reduce_over_z(terms):
    return jnp.sum(lax.all_to_all(terms, "z", 0, 0, tiled=True), axis=0)


def gather_rows(piece):
    copies = jnp.broadcast_to(piece[None], (X * C * Y, *piece.shape))
    gathered = lax.all_to_all(copies, SPREAD, 0, 0, tiled=True)
    return gathered.reshape(-1, piece.shape[1])


def gather_y(piece):
    copies = jnp.broadcast_to(piece[None], (Y, *piece.shape))
    return lax.all_to_all(copies, "y", 0, 0, tiled=True).reshape(-1, piece.shape[1])


def shift_y(value, step):
    return lax.ppermute(value, "y", [(y, (y + step) % Y) for y in range(Y)])


def shift_z(value, step):
    return lax.ppermute(value, "z", [(z, (z + step) % Z) for z in range(Z)])


def shift_far(value):
    pairs = [
        (c * Z + z, c * Z + (z + (2 if c else -2)) % Z) for c in range(C) for z in range(Z)
    ]
    return lax.ppermute(value, ("c", "z"), pairs)


def factor_over_y(factor, y):
    rows, width = factor.shape[0], factor.shape[1] // (QUAD * Y)
    blocks = factor.reshape(rows, QUAD, Y, width)
    merged = jnp.zeros((QUAD, Y * rows, width), factor.dtype)
    for step in range(Y):
        block = lax.dynamic_index_in_dim(blocks, (y + step) % Y, 2, keepdims=False)
        block = block.transpose(1, 0, 2)
        if step:
            block = shift_y(block, step)
        merged = lax.dynamic_update_slice_in_dim(merged, block, ((y - step) % Y) * rows, 1)
    return merged


def window(merged, z, core):
    pick = lambda k: lax.dynamic_index_in_dim(merged, k % QUAD, 0, keepdims=False)
    return jnp.concatenate(
        [pick(z), shift_z(pick(z + 1), 1), shift_z(pick(z - 1), -1), shift_far(pick(z + 2))], axis=0
    )


def window_of_solved(rows):
    return jnp.concatenate(
        [rows, shift_z(rows, 1), shift_z(rows, -1), shift_far(rows)], axis=1
    )


def body(panel_rhs, diag_inv, coupling, trail_factor, trail_rhs):
    core, z, y = lax.axis_index("c"), lax.axis_index("z"), lax.axis_index("y")
    prow = lax.axis_index("x") * C + core
    strip, narrow = panel_rhs.shape[0], panel_rhs.shape[2]

    rhs = lax.all_to_all(panel_rhs, "y", 0, 2, tiled=True)
    blocked = lambda m: m.reshape(m.shape[0], Z, -1)
    inv_first = blocked(gather_y(diag_inv[0]))
    couple = blocked(gather_y(coupling))
    inv_second = blocked(gather_y(diag_inv[1]))

    first = reduce_over_z(einsum("rk,kzc->zrc", rhs[:, 0], inv_first))
    second = rhs[:, 1] - reduce_over_z(einsum("rk,kzc->zrc", first, couple))
    latter = reduce_over_z(einsum("rk,kzc->zrc", second, inv_second))

    first_all = gather_rows(first)
    latter_all = gather_rows(latter)
    own = lambda rows: lax.dynamic_slice(rows, (prow * strip, y * narrow), (strip, narrow))
    solved = jnp.stack([own(first_all), own(latter_all)], axis=1)

    factor_first = window(factor_over_y(trail_factor[0], y), z, core)
    factor_latter = window(factor_over_y(trail_factor[1], y), z, core)
    update = einsum("rk,kc->rc", window_of_solved(first_all), factor_first, lax.Precision.HIGH)
    update = update + einsum("rk,kc->rc", window_of_solved(latter_all), factor_latter, lax.Precision.HIGH)

    parts = lax.all_to_all(update.reshape(Z * Y, -1, update.shape[1]), COLS, 0, 0, tiled=True)
    parts = parts.reshape(2, QUAD * Y, *parts.shape[1:])
    total = (parts[0] + parts[1]).transpose(1, 0, 2).reshape(trail_rhs.shape)
    return solved, trail_rhs - total


def solution(mesh):
    devices = Mesh(mesh.devices.reshape(X, C, Z, Y), ("x", "c", "z", "y"))
    placed = (
        P(ROWS, None, COLS),
        P(None, COLS, None),
        P(COLS, None),
        P(None, COLS, ROWS),
        P(COLS, ROWS),
    )
    return jax.shard_map(
        body,
        mesh=devices,
        in_specs=placed,
        out_specs=(P(ROWS, None, COLS), P(COLS, ROWS)),
        check_vma=False,
    )
```

```python
import functools

import jax
import jax.numpy as jnp
from jax import lax
from jax.experimental import pallas as pl
from jax.experimental.pallas import tpu as pltpu
from jax.sharding import Mesh, PartitionSpec as P

X, C, Z, Y = 4, 2, 8, 4
ROWS = ("x", "c")
COLS = ("z", "y")
SPREAD = ("x", "c", "y")
QUAD = 4
NEAR = (0, -1, 1, 2, -2)
VMEM = pl.BlockSpec(memory_space=pltpu.VMEM)
ANY = pl.BlockSpec(memory_space=pl.ANY)
SMEM = pl.BlockSpec(memory_space=pltpu.SMEM)


def f32(*shape):
    return jax.ShapeDtypeStruct(shape, jnp.float32)


def call(kernel, outs, ins, out_specs, in_specs, scratch=(), flops=0, moved=0, limit=16):
    return pl.pallas_call(
        kernel,
        out_shape=outs,
        in_specs=in_specs,
        out_specs=out_specs,
        scratch_shapes=scratch,
        compiler_params=pltpu.CompilerParams(vmem_limit_bytes=limit << 20),
        cost_estimate=pl.CostEstimate(flops=flops, bytes_accessed=moved, transcendentals=0),
    )(*ins)


def exact_dot(left, right):
    return lax.dot_general(
        left, right, (((1,), (0,)), ((), ())),
        precision=lax.Precision.HIGHEST, preferred_element_type=jnp.float32,
    )


def split(value):
    high = value.astype(jnp.bfloat16)
    return high, (value - high.astype(jnp.float32)).astype(jnp.bfloat16)


def copy_all(copies, sems):
    started = [pltpu.make_async_copy(src, dst, sems.at[i]) for i, (src, dst) in enumerate(copies)]
    for copy in started:
        copy.start()
    for copy in started:
        copy.wait()


def open_kernel(first_rhs, second_rhs, inverse, couple, terms, shared):
    product = exact_dot(first_rhs[...], inverse[0])
    rows = first_rhs.shape[0] // Y
    for z in range(Z):
        for y in range(Y):
            terms[z * Y + y] = product[y * rows:(y + 1) * rows, z * 128:(z + 1) * 128]
    for y in range(Y):
        shared[y, 0:32] = couple[...]
        shared[y, 32:64] = inverse[1]
        shared[y, 64:72] = jnp.zeros((8, shared.shape[2]), jnp.float32)
        shared[y, 64:72, 0:128] = second_rhs[y * rows:y * rows + 8]
        shared[y, 64:72, 128:256] = second_rhs[y * rows + 8:(y + 1) * rows]


def couple_kernel(arrived, shared, first, terms):
    total = jnp.sum(arrived[...], axis=0)
    first[...] = total
    product = exact_dot(total, shared[:, 0:32].reshape(128, -1))
    for z in range(Z):
        terms[z] = product[:, z * 128:(z + 1) * 128]


def latter_kernel(arrived, shared, *refs):
    terms = refs[-1]
    rhs = jnp.concatenate(
        [jnp.sum(shared[:, 64:72, 0:128], axis=0), jnp.sum(shared[:, 64:72, 128:256], axis=0)], axis=0
    )
    second = rhs - jnp.sum(arrived[...], axis=0)
    product = exact_dot(second, shared[:, 32:64].reshape(128, -1))
    part = lambda z: product[:, (z % Z) * 128:(z % Z + 1) * 128]
    for z in range(Z):
        for k, step in enumerate(NEAR):
            terms[z, k] = part(z + step)


def close_kernel(arrived, copies):
    hand_out(jnp.sum(arrived[...], axis=0), copies)


def hand_out(near, copies):
    for place in range(X * C * Y):
        copies[place, 0:3] = near[0:3]
        copies[place, 3] = near[3 + place // Y % C]


def spread_kernel(*refs):
    hand_out(jnp.stack([near[...] for near in refs[:-1]]), refs[-1])


def around(z):
    return (z % QUAD, (z + 1) % QUAD, (z + 3) % QUAD, (z + 2) % QUAD)


def cut_kernel(place, factor, *refs):
    by_class, by_y, sems = refs[:4], refs[4], refs[5]
    z, y = place[1], place[2]
    classes = around(z)
    width = by_y.shape[3]
    copies = []
    for r in range(Y):
        for k in range(QUAD):
            strip = pl.multiple_of((((y + r) % Y) * QUAD + classes[k]) * width, width)
            copies.append((factor.at[0, :, pl.ds(strip, width)], by_class[k].at[r]))
            copies.append((factor.at[1, :, pl.ds(strip, width)], by_y.at[(y + r) % Y, k]))
    copy_all(copies, sems)


def turn_kernel(*refs):
    arrived, sent, sems = refs[:4], refs[4:8], refs[8]
    copy_all([(arrived[k].at[r], sent[r].at[k]) for r in range(Y) for k in range(QUAD)], sems)


def merge_kernel(arrived, *refs):
    sent, sems = refs[:4], refs[4]
    copy_all([(arrived.at[y, k], sent[k].at[y]) for y in range(Y) for k in range(QUAD)], sems)


def multiply(rows, factor, out, acc):
    left = jnp.concatenate([rows[:, k].reshape(-1, 128) for k in range(QUAD)], axis=1)
    left_high, left_low = split(left)
    right_high, right_low = split(factor[...].reshape(left.shape[1], -1))
    dot = functools.partial(jnp.dot, preferred_element_type=jnp.float32)
    step = 128
    for top in range(0, left.shape[0], step):
        at = slice(top, top + step)
        product = dot(left_high[at], right_high) + (dot(left_high[at], right_low) + dot(left_low[at], right_high))
        blocks = slice(top // 16, (top + step) // 16)
        product = product.reshape(step // 16, 16, -1)
        out[blocks] = product if acc is None else product + acc[blocks]


def first_update_kernel(place, rows, *refs):
    arrived, out, factor, sems = refs[:4], refs[4], refs[5], refs[6]
    y = place[2]
    copy_all([(arrived[r], factor.at[:, (y + Y - r) % Y]) for r in range(Y)], sems)
    multiply(rows, factor, out, None)


def latter_update_kernel(rows, acc, *refs):
    arrived, out, factor, sems = refs[:4], refs[4], refs[5], refs[6]
    copy_all([(arrived[k], factor.at[k]) for k in range(QUAD)], sems)
    multiply(rows, factor, out, acc)


def shift_y(value, step):
    return lax.ppermute(value, "y", [(y, (y + step) % Y) for y in range(Y)])


def shift_z(value, step):
    return lax.ppermute(value, "z", [(z, (z + step) % Z) for z in range(Z)])


def shift_far(value):
    pairs = [
        (c * Z + z, c * Z + (z + (2 if c else -2)) % Z) for c in range(C) for z in range(Z)
    ]
    return lax.ppermute(value, ("c", "z"), pairs)


def to_windows(own, up, down, far):
    return own, shift_z(up, 1), shift_z(down, -1), shift_far(far)


def to_ys(own, *others):
    return own, *(shift_y(other, step + 1) for step, other in enumerate(others))


def exchange(value, axes):
    return lax.all_to_all(value, axes, 0, 0, tiled=True)


def body(panel_rhs, diag_inv, coupling, trail_factor, trail_rhs):
    core, z, y = lax.axis_index("c"), lax.axis_index("z"), lax.axis_index("y")
    prow = lax.axis_index("x") * C + core
    place = jnp.stack([core, z, y]).astype(jnp.int32)
    strip, narrow = panel_rhs.shape[0], panel_rhs.shape[2]
    width = trail_rhs.shape[1] // (QUAD * Y)
    block = f32(QUAD, 32, width)
    sems = lambda n: [pltpu.SemaphoreType.DMA((n,))]

    rhs = panel_rhs.transpose(1, 0, 2)
    lanes = lax.broadcasted_iota(jnp.int32, (1, 128), 1) // narrow
    second_rhs = jnp.where(lanes == y, jnp.tile(rhs[1], (1, Y)), 0.0)
    terms, shared = call(
        open_kernel, (f32(Z * Y, 16, 128), f32(Y, 72, 1024)),
        (rhs[0], second_rhs, diag_inv, coupling), (VMEM, VMEM), (VMEM,) * 4,
    )
    arrived = exchange(terms, COLS)
    shared = exchange(shared, "y")

    *by_class, by_y = call(
        cut_kernel, (block,) * 4 + (f32(Y, *block.shape),), (place, trail_factor),
        (ANY,) * 5, (SMEM, VMEM), sems(32), moved=7340032, limit=24,
    )
    by_class = to_windows(*by_class)
    by_y = exchange(by_y, "y")

    first, terms = call(couple_kernel, (f32(16, 128), f32(Z, 16, 128)), (arrived, shared), (VMEM, VMEM), (VMEM,) * 2)
    arrived = exchange(terms, "z")
    terms = call(latter_kernel, f32(Z, len(NEAR), 16, 128), (arrived, shared, *by_class[1:], by_y), VMEM, (VMEM, VMEM) + (ANY,) * 4)
    arrived = exchange(terms, "z")
    copies = call(close_kernel, f32(X * C * Y, QUAD, 16, 128), (arrived,), VMEM, (VMEM,))
    latter_rows = exchange(copies, SPREAD)

    near = (first, *(shift_z(first, -step) for step in NEAR[1:]))
    copies = call(spread_kernel, f32(X * C * Y, QUAD, 16, 128), near, VMEM, (VMEM,) * len(NEAR))
    first_rows = exchange(copies, SPREAD)

    by_r = call(turn_kernel, (block,) * 4, by_class, (ANY,) * 4, (VMEM,) * 4, sems(16), moved=3670016)
    first_factor = to_ys(*by_r)
    by_k = call(merge_kernel, (block,) * 4, (by_y,), (ANY,) * 4, (VMEM,), sems(16), moved=3670016)
    latter_factor = to_windows(*by_k)

    scratch = [pltpu.VMEM((QUAD, Y, 32, width), jnp.float32)] + sems(4)
    update = call(
        first_update_kernel, f32(Z * Y, 16, width), (place, first_rows, *first_factor),
        VMEM, (SMEM, VMEM) + (ANY,) * 4, scratch, flops=1409286144, moved=4718592, limit=40,
    )
    scratch = [pltpu.VMEM((QUAD, QUAD, 32, width), jnp.float32)] + sems(4)
    update = call(
        latter_update_kernel, f32(Z * Y, 16, width), (latter_rows, update, *latter_factor),
        VMEM, (VMEM,) * 2 + (ANY,) * 4, scratch, flops=1409286144, moved=6553600, limit=40,
    )
    parts = exchange(update, COLS)
    parts = parts.reshape(2, QUAD, Y, *parts.shape[1:])
    reduced = trail_rhs - (parts[0] + parts[1]).transpose(2, 1, 0, 3).reshape(trail_rhs.shape)

    own = lambda rows: lax.dynamic_slice(
        rows, (prow * Y, 0, 0, y * narrow), (Y, 1, rows.shape[2], narrow)
    ).reshape(strip, narrow)
    solved = jnp.stack([own(first_rows), own(latter_rows)], axis=1)
    return solved, reduced


def solution(mesh):
    devices = Mesh(mesh.devices.reshape(X, C, Z, Y), ("x", "c", "z", "y"))
    placed = (
        P(ROWS, None, COLS),
        P(None, COLS, None),
        P(COLS, None),
        P(None, COLS, ROWS),
        P(COLS, ROWS),
    )
    return jax.shard_map(
        body,
        mesh=devices,
        in_specs=placed,
        out_specs=(P(ROWS, None, COLS), P(COLS, ROWS)),
        check_vma=False,
    )
```

```python
import functools

import jax
import jax.numpy as jnp
from jax import lax
from jax.experimental import pallas as pl
from jax.experimental.pallas import tpu as pltpu
from jax.sharding import Mesh, PartitionSpec as P

X, C, Z, Y = 4, 2, 8, 4
ROWS = ("x", "c")
COLS = ("z", "y")
SPREAD = ("x", "c", "y")
QUAD = 4
NEAR = (0, -1, 1, 2, -2)
VMEM = pl.BlockSpec(memory_space=pltpu.VMEM)
ANY = pl.BlockSpec(memory_space=pl.ANY)
SMEM = pl.BlockSpec(memory_space=pltpu.SMEM)


def f32(*shape):
    return jax.ShapeDtypeStruct(shape, jnp.float32)


def call(kernel, outs, ins, out_specs, in_specs, scratch=(), flops=0, moved=0, limit=16):
    return pl.pallas_call(
        kernel,
        out_shape=outs,
        in_specs=in_specs,
        out_specs=out_specs,
        scratch_shapes=scratch,
        compiler_params=pltpu.CompilerParams(vmem_limit_bytes=limit << 20),
        cost_estimate=pl.CostEstimate(flops=flops, bytes_accessed=moved, transcendentals=0),
    )(*ins)


def exact_dot(left, right):
    return lax.dot_general(
        left, right, (((1,), (0,)), ((), ())),
        precision=lax.Precision.HIGHEST, preferred_element_type=jnp.float32,
    )


def split(value):
    high = value.astype(jnp.bfloat16)
    return high, (value - high.astype(jnp.float32)).astype(jnp.bfloat16)


def copy_all(copies, sems):
    started = [pltpu.make_async_copy(src, dst, sems.at[i]) for i, (src, dst) in enumerate(copies)]
    for copy in started:
        copy.start()
    for copy in started:
        copy.wait()


def open_kernel(first_rhs, second_rhs, inverse, couple, terms, shared):
    product = exact_dot(first_rhs[...], inverse[0])
    rows = first_rhs.shape[0] // Y
    for z in range(Z):
        for y in range(Y):
            terms[z * Y + y] = product[y * rows:(y + 1) * rows, z * 128:(z + 1) * 128]
    for y in range(Y):
        shared[y, 0:32] = couple[...]
        shared[y, 32:64] = inverse[1]
        shared[y, 64:72] = jnp.zeros((8, shared.shape[2]), jnp.float32)
        shared[y, 64:72, 0:128] = second_rhs[y * rows:y * rows + 8]
        shared[y, 64:72, 128:256] = second_rhs[y * rows + 8:(y + 1) * rows]


def couple_kernel(arrived, shared, *refs):
    first, terms = refs[-2:]
    total = jnp.sum(arrived[...], axis=0)
    first[...] = total
    product = exact_dot(total, shared[:, 0:32].reshape(128, -1))
    for z in range(Z):
        terms[z] = product[:, z * 128:(z + 1) * 128]


def latter_kernel(arrived, shared, terms):
    rhs = jnp.concatenate(
        [jnp.sum(shared[:, 64:72, 0:128], axis=0), jnp.sum(shared[:, 64:72, 128:256], axis=0)], axis=0
    )
    second = rhs - jnp.sum(arrived[...], axis=0)
    product = exact_dot(second, shared[:, 32:64].reshape(128, -1))
    part = lambda z: product[:, (z % Z) * 128:(z % Z + 1) * 128]
    for z in range(Z):
        for k, step in enumerate(NEAR):
            terms[z, k] = part(z + step)


def close_kernel(arrived, *refs):
    hand_out(jnp.sum(arrived[...], axis=0), refs[-1])


def hand_out(near, copies):
    for place in range(X * C * Y):
        copies[place, 0:3] = near[0:3]
        copies[place, 3] = near[3 + place // Y % C]


def spread_kernel(*refs):
    hand_out(jnp.stack([near[...] for near in refs[:-1]]), refs[-1])


def around(z):
    return (z % QUAD, (z + 1) % QUAD, (z + 3) % QUAD, (z + 2) % QUAD)


def cut_kernel(place, factor, *refs):
    by_class, by_y, sems = refs[:4], refs[4], refs[5]
    classes = around(place[0])
    width = by_y.shape[3]
    copies = []
    for y in range(Y):
        for k in range(QUAD):
            strip = pl.ds(pl.multiple_of((y * QUAD + classes[k]) * width, width), width)
            copies.append((factor.at[0, :, strip], by_class[k].at[y]))
            copies.append((factor.at[1, :, strip], by_y.at[y, k]))
    copy_all(copies, sems)


def turn_kernel(*refs):
    arrived, sent, sems = refs[:4], refs[4], refs[5]
    copy_all([(arrived[k].at[y], sent.at[y, k]) for y in range(Y) for k in range(QUAD)], sems)


def merge_kernel(arrived, *refs):
    sent, sems = refs[:4], refs[4]
    copy_all([(arrived.at[y, k], sent[k].at[y]) for y in range(Y) for k in range(QUAD)], sems)


def update_kernel(count, *refs):
    rows, blocks, acc = refs[0], refs[1:1 + count], refs[1 + count:-5]
    out, left, factor, result, sems = refs[-5:]
    start = lambda src, dst, i: pltpu.make_async_copy(src, dst, sems.at[i])
    chunk = 128 // 16
    steps = left.shape[0] // chunk
    part = lambda i: slice(i * chunk, (i + 1) * chunk)
    rows_in = start(rows, left, 0)
    rows_in.start()
    if count == 1:
        factor_in = [start(blocks[0].at[:, k], factor.at[k], 1 + k) for k in range(QUAD)]
    else:
        factor_in = [start(blocks[k], factor.at[k], 1 + k) for k in range(QUAD)]
    for copy in factor_in:
        copy.start()
    acc_in = [start(a.at[part(i)], result.at[part(i)], 5 + i) for a in acc for i in range(steps)]
    for copy in acc_in:
        copy.start()
    rows_in.wait()
    for copy in factor_in:
        copy.wait()
    right_high, right_low = split(factor[...].reshape(QUAD * 128, -1))
    dot = functools.partial(jnp.dot, preferred_element_type=jnp.float32)
    sent = []
    for i in range(steps):
        piece = left[part(i)]
        high, low = split(jnp.concatenate([piece[:, k].reshape(128, 128) for k in range(QUAD)], axis=1))
        product = dot(high, right_high) + (dot(high, right_low) + dot(low, right_high))
        product = product.reshape(chunk, 16, -1)
        if acc:
            acc_in[i].wait()
            product = product + result[part(i)]
        result[part(i)] = product
        sent.append(start(result.at[part(i)], out.at[part(i)], 5 + steps + i))
        sent[-1].start()
    for copy in sent:
        copy.wait()


def update_call(rows, blocks, acc=()):
    width = blocks[0].shape[-1]
    count = X * C * Y
    steps = count * 16 // 128
    return call(
        functools.partial(update_kernel, len(blocks)), f32(count, 16, width), (rows, *blocks, *acc),
        ANY, (ANY,) * (1 + len(blocks) + len(acc)),
        [
            pltpu.VMEM(rows.shape, jnp.float32),
            pltpu.VMEM((QUAD, Y, 32, width), jnp.float32),
            pltpu.VMEM((count, 16, width), jnp.float32),
            pltpu.SemaphoreType.DMA((5 + 2 * steps,)),
        ],
        flops=1409286144, moved=4718592, limit=60,
    )


def shift_z(value, step):
    return lax.ppermute(value, "z", [(z, (z + step) % Z) for z in range(Z)])


def shift_far(value):
    pairs = [
        (c * Z + z, c * Z + (z + (2 if c else -2)) % Z) for c in range(C) for z in range(Z)
    ]
    return lax.ppermute(value, ("c", "z"), pairs)


def to_windows(own, up, down, far):
    return own, shift_z(up, 1), shift_z(down, -1), shift_far(far)


def exchange(value, axes):
    return lax.all_to_all(value, axes, 0, 0, tiled=True)


def body(panel_rhs, diag_inv, coupling, trail_factor, trail_rhs):
    z, y = lax.axis_index("z"), lax.axis_index("y")
    prow = lax.axis_index("x") * C + lax.axis_index("c")
    strip, narrow = panel_rhs.shape[0], panel_rhs.shape[2]
    width = trail_rhs.shape[1] // (QUAD * Y)
    block = f32(QUAD, 32, width)
    sems = lambda n: [pltpu.SemaphoreType.DMA((n,))]

    rhs = panel_rhs.transpose(1, 0, 2)
    lanes = lax.broadcasted_iota(jnp.int32, (1, 128), 1) // narrow
    second_rhs = jnp.where(lanes == y, jnp.tile(rhs[1], (1, Y)), 0.0)
    terms, shared = call(
        open_kernel, (f32(Z * Y, 16, 128), f32(Y, 72, 1024)),
        (rhs[0], second_rhs, diag_inv, coupling), (VMEM, VMEM), (VMEM,) * 4,
    )
    arrived = exchange(terms, COLS)
    shared = exchange(shared, "y")

    *by_class, by_y = call(
        cut_kernel, (block,) * 4 + (f32(Y, *block.shape),), (z.astype(jnp.int32).reshape(1), trail_factor),
        (ANY,) * 5, (SMEM, VMEM), sems(32), moved=7340032, limit=60,
    )
    by_class = to_windows(*by_class)
    by_y = exchange(by_y, "y")

    first, terms = call(
        couple_kernel, (f32(16, 128), f32(Z, 16, 128)), (arrived, shared, *by_class[1:], by_y),
        (VMEM, VMEM), (VMEM, VMEM) + (ANY,) * 4,
    )
    arrived = exchange(terms, "z")
    turned = call(turn_kernel, f32(Y, *block.shape), by_class, ANY, (VMEM,) * 4, sems(16), moved=3670016, limit=60)
    first_factor = exchange(turned, "y")
    by_k = call(merge_kernel, (block,) * 4, (by_y,), (ANY,) * 4, (VMEM,), sems(16), moved=3670016, limit=60)
    latter_factor = to_windows(*by_k)

    near = (first, *(shift_z(first, -step) for step in NEAR[1:]))
    copies = call(spread_kernel, f32(X * C * Y, QUAD, 16, 128), near, VMEM, (VMEM,) * len(NEAR))
    first_rows = exchange(copies, SPREAD)

    terms = call(latter_kernel, f32(Z, len(NEAR), 16, 128), (arrived, shared), VMEM, (VMEM, VMEM))
    arrived = exchange(terms, "z")
    copies = call(
        close_kernel, f32(X * C * Y, QUAD, 16, 128), (arrived, first_factor, by_k[0]), VMEM, (VMEM, ANY, ANY)
    )
    latter_rows = exchange(copies, SPREAD)

    update = update_call(first_rows, (first_factor,))
    update = update_call(latter_rows, latter_factor, (update,))
    parts = exchange(update, COLS)
    parts = parts.reshape(2, QUAD, Y, *parts.shape[1:])
    reduced = trail_rhs - (parts[0] + parts[1]).transpose(2, 1, 0, 3).reshape(trail_rhs.shape)

    own = lambda rows: lax.dynamic_slice(
        rows, (prow * Y, 0, 0, y * narrow), (Y, 1, rows.shape[2], narrow)
    ).reshape(strip, narrow)
    solved = jnp.stack([own(first_rows), own(latter_rows)], axis=1)
    return solved, reduced


def solution(mesh):
    devices = Mesh(mesh.devices.reshape(X, C, Z, Y), ("x", "c", "z", "y"))
    placed = (
        P(ROWS, None, COLS),
        P(None, COLS, None),
        P(COLS, None),
        P(None, COLS, ROWS),
        P(COLS, ROWS),
    )
    return jax.shard_map(
        body,
        mesh=devices,
        in_specs=placed,
        out_specs=(P(ROWS, None, COLS), P(COLS, ROWS)),
        check_vma=False,
    )
```

```python
import functools

import jax
import jax.numpy as jnp
from jax import lax
from jax.experimental import pallas as pl
from jax.experimental.pallas import tpu as pltpu
from jax.sharding import Mesh, PartitionSpec as P

X, C, Z, Y = 4, 2, 8, 4
ROWS = ("x", "c")
COLS = ("z", "y")
SPREAD = ("x", "c", "y")
QUAD = 4
NEAR = (0, -1, 1, 2, -2)
VMEM = pl.BlockSpec(memory_space=pltpu.VMEM)
ANY = pl.BlockSpec(memory_space=pl.ANY)
SMEM = pl.BlockSpec(memory_space=pltpu.SMEM)


def f32(*shape):
    return jax.ShapeDtypeStruct(shape, jnp.float32)


def call(kernel, outs, ins, out_specs, in_specs, scratch=(), flops=0, moved=0, limit=16):
    return pl.pallas_call(
        kernel,
        out_shape=outs,
        in_specs=in_specs,
        out_specs=out_specs,
        scratch_shapes=scratch,
        compiler_params=pltpu.CompilerParams(vmem_limit_bytes=limit << 20),
        cost_estimate=pl.CostEstimate(flops=flops, bytes_accessed=moved, transcendentals=0),
    )(*ins)


def exact_dot(left, right):
    return lax.dot_general(
        left, right, (((1,), (0,)), ((), ())),
        precision=lax.Precision.HIGHEST, preferred_element_type=jnp.float32,
    )


def split(value):
    high = value.astype(jnp.bfloat16)
    return high, (value - high.astype(jnp.float32)).astype(jnp.bfloat16)


def copy_all(copies, sems):
    started = [pltpu.make_async_copy(src, dst, sems.at[i]) for i, (src, dst) in enumerate(copies)]
    for copy in started:
        copy.start()
    for copy in started:
        copy.wait()


def open_kernel(rhs, inverse, terms):
    product = exact_dot(rhs[...], inverse[0])
    rows = rhs.shape[0] // Y
    for z in range(Z):
        for y in range(Y):
            terms[z * Y + y] = product[y * rows:(y + 1) * rows, z * 128:(z + 1) * 128]


def share_kernel(place, rhs, inverse, couple, *shared):
    for r in range(Y):
        rows = pl.ds(pl.multiple_of((place[1] + r) % Y * 16, 16), 16)
        piece = rhs[rows]
        shared[r][0:32] = couple[...]
        shared[r][32:64] = inverse[1]
        shared[r][64:72] = jnp.zeros((8, shared[r].shape[1]), jnp.float32)
        shared[r][64:72, 0:128] = piece[0:8]
        shared[r][64:72, 128:256] = piece[8:16]


def in_order(place, shared, rows, matrix):
    for r in range(Y):
        matrix[(place[1] + Y - r) % Y] = shared[r][rows]
    return matrix[...].reshape(Y * 32, -1)


def couple_kernel(place, arrived, *refs):
    shared, (first, terms, matrix) = refs[:Y], refs[-3:]
    total = jnp.sum(arrived[...], axis=0)
    first[...] = total
    product = exact_dot(total, in_order(place, shared, slice(0, 32), matrix))
    for z in range(Z):
        terms[z] = product[:, z * 128:(z + 1) * 128]


def latter_kernel(place, arrived, *refs):
    shared, (terms, matrix) = refs[:Y], refs[-2:]
    rhs = sum(piece[64:72] for piece in shared)
    rhs = jnp.concatenate([rhs[:, 0:128], rhs[:, 128:256]], axis=0)
    second = rhs - jnp.sum(arrived[...], axis=0)
    product = exact_dot(second, in_order(place, shared, slice(32, 64), matrix))
    part = lambda z: product[:, (z % Z) * 128:(z % Z + 1) * 128]
    for z in range(Z):
        for k, step in enumerate(NEAR):
            terms[z, k] = part(z + step)


def close_kernel(arrived, *refs):
    latter = jnp.sum(arrived[...], axis=0)
    first, copies = refs[:-1], refs[-1]
    for place in range(X * C * Y):
        for k in range(QUAD):
            near = k if k < 3 else 3 + place // Y % C
            copies[place, k] = first[near][...]
            copies[place, QUAD + k] = latter[near]


def around(z):
    return (z % QUAD, (z + 1) % QUAD, (z + 3) % QUAD, (z + 2) % QUAD)


def cut_kernel(place, factor, *refs):
    by_class, by_y, sems = refs[:4], refs[4:8], refs[8]
    classes = around(place[0])
    width = by_y[0].shape[2]
    copies = []
    for r in range(Y):
        for k in range(QUAD):
            strip = pl.multiple_of(((place[1] + r) % Y * QUAD + classes[k]) * width, width)
            copies.append((factor.at[0, :, pl.ds(strip, width)], by_class[k].at[r]))
            copies.append((factor.at[1, :, pl.ds(strip, width)], by_y[r].at[k]))
    copy_all(copies, sems)


def turn_kernel(*refs):
    arrived, sent, sems = refs[:4], refs[4:8], refs[8]
    copy_all([(arrived[k].at[r], sent[r].at[k]) for r in range(Y) for k in range(QUAD)], sems)


def merge_kernel(place, *refs):
    arrived, sent, sems = refs[:4], refs[4:8], refs[8]
    copy_all([(arrived[r].at[k], sent[k].at[(place[1] + Y - r) % Y]) for r in range(Y) for k in range(QUAD)], sems)


def update_kernel(place, rows, *refs):
    by_r, by_k = refs[:Y], refs[Y:Y + QUAD]
    out, left, factor, result, sems = refs[-5:]
    start = lambda src, dst, i: pltpu.make_async_copy(src, dst, sems.at[i])
    chunk = 128 // 16
    part = lambda i: slice(i * chunk, (i + 1) * chunk)
    arriving = [start(rows, left, 0)]
    arriving += [start(by_r[r], factor.at[0, :, (place[1] + Y - r) % Y], 1 + r) for r in range(Y)]
    arriving += [start(by_k[k], factor.at[1, k], 1 + Y + k) for k in range(QUAD)]
    for copy in arriving:
        copy.start()
    for copy in arriving:
        copy.wait()
    right_high, right_low = split(factor[...].reshape(2 * QUAD * 128, -1))
    dot = functools.partial(jnp.dot, preferred_element_type=jnp.float32)
    sent = []
    for i in range(left.shape[0] // chunk):
        piece = left[part(i)]
        high, low = split(jnp.concatenate([piece[:, k].reshape(128, 128) for k in range(2 * QUAD)], axis=1))
        product = dot(high, right_high) + (dot(high, right_low) + dot(low, right_high))
        result[part(i)] = product.reshape(chunk, 16, -1)
        sent.append(start(result.at[part(i)], out.at[part(i)], 1 + Y + QUAD + i))
        sent[-1].start()
    for copy in sent:
        copy.wait()


def shift_y(value, step):
    return lax.ppermute(value, "y", [(y, (y + step) % Y) for y in range(Y)])


def shift_z(value, step):
    return lax.ppermute(value, "z", [(z, (z + step) % Z) for z in range(Z)])


def shift_far(value):
    pairs = [
        (c * Z + z, c * Z + (z + (2 if c else -2)) % Z) for c in range(C) for z in range(Z)
    ]
    return lax.ppermute(value, ("c", "z"), pairs)


def to_windows(own, up, down, far):
    return own, shift_z(up, 1), shift_z(down, -1), shift_far(far)


def to_ys(own, *others):
    return own, *(shift_y(other, step + 1) for step, other in enumerate(others))


def exchange(value, axes):
    return lax.all_to_all(value, axes, 0, 0, tiled=True)


def body(panel_rhs, diag_inv, coupling, trail_factor, trail_rhs):
    z, y = lax.axis_index("z"), lax.axis_index("y")
    prow = lax.axis_index("x") * C + lax.axis_index("c")
    place = jnp.stack([z, y]).astype(jnp.int32)
    strip, narrow = panel_rhs.shape[0], panel_rhs.shape[2]
    width = trail_rhs.shape[1] // (QUAD * Y)
    block = f32(QUAD, 32, width)
    sems = lambda n: [pltpu.SemaphoreType.DMA((n,))]
    matrix = [pltpu.VMEM((Y, 32, 1024), jnp.float32)]

    rhs = panel_rhs.transpose(1, 0, 2)
    lanes = lax.broadcasted_iota(jnp.int32, (1, 128), 1) // narrow
    second_rhs = jnp.where(lanes == y, jnp.tile(rhs[1], (1, Y)), 0.0)
    shared = call(
        share_kernel, (f32(72, 1024),) * Y, (place, second_rhs, diag_inv, coupling),
        (VMEM,) * Y, (SMEM,) + (VMEM,) * 3,
    )
    shared = to_ys(*shared)
    terms = call(open_kernel, f32(Z * Y, 16, 128), (rhs[0], diag_inv), VMEM, (VMEM,) * 2)
    arrived = exchange(terms, COLS)

    cut = call(
        cut_kernel, (block,) * 8, (place, trail_factor), (ANY,) * 8, (SMEM, VMEM), sems(32), moved=7340032, limit=60,
    )
    by_class, by_y = to_windows(*cut[:4]), to_ys(*cut[4:])

    first, terms = call(
        couple_kernel, (f32(16, 128), f32(Z, 16, 128)), (place, arrived, *shared, *by_class[1:]),
        (VMEM, VMEM), (SMEM,) + (VMEM,) * 5 + (ANY,) * 3, matrix,
    )
    arrived = exchange(terms, "z")
    by_r = call(turn_kernel, (block,) * 4, by_class, (ANY,) * 4, (VMEM,) * 4, sems(16), moved=3670016, limit=60)
    first_factor = to_ys(*by_r)
    near = (first, *(shift_z(first, -step) for step in NEAR[1:]))

    terms = call(
        latter_kernel, f32(Z, len(NEAR), 16, 128), (place, arrived, *shared, *by_y[1:]),
        VMEM, (SMEM,) + (VMEM,) * 5 + (ANY,) * 3, matrix,
    )
    arrived = exchange(terms, "z")
    by_k = call(merge_kernel, (block,) * 4, (place, *by_y), (ANY,) * 4, (SMEM,) + (VMEM,) * 4, sems(16), moved=3670016, limit=60)
    latter_factor = to_windows(*by_k)
    copies = call(close_kernel, f32(X * C * Y, 2 * QUAD, 16, 128), (arrived, *near), VMEM, (VMEM,) * 6)
    rows = exchange(copies, SPREAD)

    update = call(
        update_kernel, f32(X * C * Y, 16, width), (place, rows, *first_factor, *latter_factor),
        ANY, (SMEM,) + (ANY,) * 9,
        [
            pltpu.VMEM(rows.shape, jnp.float32),
            pltpu.VMEM((2, QUAD, Y, 32, width), jnp.float32),
            pltpu.VMEM((X * C * Y, 16, width), jnp.float32),
        ] + sems(17),
        flops=2818572288, moved=7602176, limit=60,
    )
    parts = exchange(update, COLS)
    parts = parts.reshape(2, QUAD, Y, *parts.shape[1:])
    reduced = trail_rhs - (parts[0] + parts[1]).transpose(2, 1, 0, 3).reshape(trail_rhs.shape)

    own = lambda panel: lax.dynamic_slice(
        rows, (prow * Y, panel * QUAD, 0, y * narrow), (Y, 1, rows.shape[2], narrow)
    ).reshape(strip, narrow)
    solved = jnp.stack([own(0), own(1)], axis=1)
    return solved, reduced


def solution(mesh):
    devices = Mesh(mesh.devices.reshape(X, C, Z, Y), ("x", "c", "z", "y"))
    placed = (
        P(ROWS, None, COLS),
        P(None, COLS, None),
        P(COLS, None),
        P(None, COLS, ROWS),
        P(COLS, ROWS),
    )
    return jax.shard_map(
        body,
        mesh=devices,
        in_specs=placed,
        out_specs=(P(ROWS, None, COLS), P(COLS, ROWS)),
        check_vma=False,
    )
```

```python
import functools

import jax
import jax.numpy as jnp
from jax import lax
from jax.experimental import pallas as pl
from jax.experimental.pallas import tpu as pltpu
from jax.sharding import Mesh, PartitionSpec as P

X, C, Z, Y = 4, 2, 8, 4
ROWS = ("x", "c")
COLS = ("z", "y")
SPREAD = ("x", "c", "y")
QUAD = 4
NEAR = (0, -1, 1, 2, -2)
VMEM = pl.BlockSpec(memory_space=pltpu.VMEM)
ANY = pl.BlockSpec(memory_space=pl.ANY)
SMEM = pl.BlockSpec(memory_space=pltpu.SMEM)


def f32(*shape):
    return jax.ShapeDtypeStruct(shape, jnp.float32)


def call(kernel, outs, ins, out_specs, in_specs, scratch=(), flops=0, moved=0, limit=16):
    return pl.pallas_call(
        kernel,
        out_shape=outs,
        in_specs=in_specs,
        out_specs=out_specs,
        scratch_shapes=scratch,
        compiler_params=pltpu.CompilerParams(vmem_limit_bytes=limit << 20),
        cost_estimate=pl.CostEstimate(flops=flops, bytes_accessed=moved, transcendentals=0),
    )(*ins)


def exact_dot(left, right):
    return lax.dot_general(
        left, right, (((1,), (0,)), ((), ())),
        precision=lax.Precision.HIGHEST, preferred_element_type=jnp.float32,
    )


def split(value):
    high = value.astype(jnp.bfloat16)
    return high, (value - high.astype(jnp.float32)).astype(jnp.bfloat16)


def copy_all(copies, sems):
    started = [pltpu.make_async_copy(src, dst, sems.at[i]) for i, (src, dst) in enumerate(copies)]
    for copy in started:
        copy.start()
    for copy in started:
        copy.wait()


def open_kernel(rhs, inverse, terms):
    product = exact_dot(rhs[...], inverse[0])
    rows = rhs.shape[0] // Y
    for z in range(Z):
        for y in range(Y):
            terms[z * Y + y] = product[y * rows:(y + 1) * rows, z * 128:(z + 1) * 128]


def share_kernel(place, rhs, inverse, couple, *shared):
    for r in range(Y):
        rows = pl.ds(pl.multiple_of((place[1] + r) % Y * 16, 16), 16)
        piece = rhs[rows]
        shared[r][0:32] = couple[...]
        shared[r][32:64] = inverse[1]
        shared[r][64:72] = jnp.zeros((8, shared[r].shape[1]), jnp.float32)
        shared[r][64:72, 0:128] = piece[0:8]
        shared[r][64:72, 128:256] = piece[8:16]


def in_order(place, shared, rows, matrix):
    for r in range(Y):
        matrix[(place[1] + Y - r) % Y] = shared[r][rows]
    return matrix[...].reshape(Y * 32, -1)


def couple_kernel(place, arrived, *refs):
    shared, (first, terms, matrix) = refs[:Y], refs[-3:]
    total = jnp.sum(arrived[...], axis=0)
    first[...] = total
    product = exact_dot(total, in_order(place, shared, slice(0, 32), matrix))
    for z in range(Z):
        terms[z] = product[:, z * 128:(z + 1) * 128]


def latter_kernel(place, arrived, *refs):
    shared, (terms, matrix) = refs[:Y], refs[-2:]
    rhs = sum(piece[64:72] for piece in shared)
    rhs = jnp.concatenate([rhs[:, 0:128], rhs[:, 128:256]], axis=0)
    second = rhs - jnp.sum(arrived[...], axis=0)
    product = exact_dot(second, in_order(place, shared, slice(32, 64), matrix))
    part = lambda z: product[:, (z % Z) * 128:(z % Z + 1) * 128]
    for z in range(Z):
        for k, step in enumerate(NEAR):
            terms[z, k] = part(z + step)


def close_kernel(arrived, *refs):
    latter = jnp.sum(arrived[...], axis=0)
    first, copies = refs[:len(NEAR)], refs[-1]
    for place in range(X * C * Y):
        for k in range(QUAD):
            near = k if k < 3 else 3 + place // Y % C
            copies[place, k] = first[near][...]
            copies[place, QUAD + k] = latter[near]


def around(z):
    return (z % QUAD, (z + 1) % QUAD, (z + 3) % QUAD, (z + 2) % QUAD)


def cut_kernel(place, factor, *refs):
    by_class, by_y, sems = refs[:4], refs[4:8], refs[8]
    classes = around(place[0])
    width = by_y[0].shape[2]
    copies = []
    for r in range(Y):
        for k in range(QUAD):
            strip = pl.multiple_of(((place[1] + r) % Y * QUAD + classes[k]) * width, width)
            copies.append((factor.at[0, :, pl.ds(strip, width)], by_class[k].at[r]))
            copies.append((factor.at[1, :, pl.ds(strip, width)], by_y[r].at[k]))
    copy_all(copies, sems)


def turn_kernel(*refs):
    arrived, sent, sems = refs[:4], refs[4:8], refs[8]
    copy_all([(arrived[k].at[r], sent[r].at[k]) for r in range(Y) for k in range(QUAD)], sems)


def merge_kernel(place, *refs):
    arrived, sent, sems = refs[:4], refs[4:8], refs[8]
    copy_all([(arrived[r].at[k], sent[k].at[(place[1] + Y - r) % Y]) for r in range(Y) for k in range(QUAD)], sems)


def update_kernel(place, rows, *refs):
    by_r, by_k = refs[:Y], refs[Y:Y + QUAD]
    out, left, factor, result, sems = refs[-5:]
    start = lambda src, dst, i: pltpu.make_async_copy(src, dst, sems.at[i])
    chunk = 128 // 16
    part = lambda i: slice(i * chunk, (i + 1) * chunk)
    arriving = [start(rows, left, 0)]
    arriving += [start(by_r[r], factor.at[0, :, (place[1] + Y - r) % Y], 1 + r) for r in range(Y)]
    arriving += [start(by_k[k], factor.at[1, k], 1 + Y + k) for k in range(QUAD)]
    for copy in arriving:
        copy.start()
    for copy in arriving:
        copy.wait()
    right_high, right_low = split(factor[...].reshape(2 * QUAD * 128, -1))
    dot = functools.partial(jnp.dot, preferred_element_type=jnp.float32)
    sent = []
    for i in range(left.shape[0] // chunk):
        piece = left[part(i)]
        high, low = split(jnp.concatenate([piece[:, k].reshape(128, 128) for k in range(2 * QUAD)], axis=1))
        product = dot(high, right_high) + (dot(high, right_low) + dot(low, right_high))
        result[part(i)] = product.reshape(chunk, 16, -1)
        sent.append(start(result.at[part(i)], out.at[part(i)], 1 + Y + QUAD + i))
        sent[-1].start()
    for copy in sent:
        copy.wait()


def shift_y(value, step):
    return lax.ppermute(value, "y", [(y, (y + step) % Y) for y in range(Y)])


def shift_z(value, step):
    return lax.ppermute(value, "z", [(z, (z + step) % Z) for z in range(Z)])


def shift_far(value):
    pairs = [
        (c * Z + z, c * Z + (z + (2 if c else -2)) % Z) for c in range(C) for z in range(Z)
    ]
    return lax.ppermute(value, ("c", "z"), pairs)


def to_windows(own, up, down, far):
    return own, shift_z(up, 1), shift_z(down, -1), shift_far(far)


def to_ys(own, *others):
    return own, *(shift_y(other, step + 1) for step, other in enumerate(others))


def exchange(value, axes):
    return lax.all_to_all(value, axes, 0, 0, tiled=True)


def body(panel_rhs, diag_inv, coupling, trail_factor, trail_rhs):
    z, y = lax.axis_index("z"), lax.axis_index("y")
    prow = lax.axis_index("x") * C + lax.axis_index("c")
    place = jnp.stack([z, y]).astype(jnp.int32)
    strip, narrow = panel_rhs.shape[0], panel_rhs.shape[2]
    width = trail_rhs.shape[1] // (QUAD * Y)
    block = f32(QUAD, 32, width)
    sems = lambda n: [pltpu.SemaphoreType.DMA((n,))]
    matrix = [pltpu.VMEM((Y, 32, 1024), jnp.float32)]

    rhs = panel_rhs.transpose(1, 0, 2)
    lanes = lax.broadcasted_iota(jnp.int32, (1, 128), 1) // narrow
    second_rhs = jnp.where(lanes == y, jnp.tile(rhs[1], (1, Y)), 0.0)
    shared = call(
        share_kernel, (f32(72, 1024),) * Y, (place, second_rhs, diag_inv, coupling),
        (VMEM,) * Y, (SMEM,) + (VMEM,) * 3,
    )
    shared = to_ys(*shared)
    terms = call(open_kernel, f32(Z * Y, 16, 128), (rhs[0], diag_inv), VMEM, (VMEM,) * 2)
    arrived = exchange(terms, COLS)

    cut = call(
        cut_kernel, (block,) * 8, (place, trail_factor), (ANY,) * 8, (SMEM, VMEM), sems(32), moved=7340032, limit=60,
    )
    by_class, by_y = to_windows(*cut[:4]), to_ys(*cut[4:])

    first, terms = call(
        couple_kernel, (f32(16, 128), f32(Z, 16, 128)), (place, arrived, *shared, cut[0], cut[4]),
        (VMEM, VMEM), (SMEM,) + (VMEM,) * 5 + (ANY,) * 2, matrix, limit=60,
    )
    arrived = exchange(terms, "z")
    by_r = call(turn_kernel, (block,) * 4, by_class, (ANY,) * 4, (VMEM,) * 4, sems(16), moved=3670016, limit=60)
    first_factor = to_ys(*by_r)
    near = (first, *(shift_z(first, -step) for step in NEAR[1:]))

    terms = call(
        latter_kernel, f32(Z, len(NEAR), 16, 128), (place, arrived, *shared, *by_class[1:], *by_y[1:]),
        VMEM, (SMEM,) + (VMEM,) * 5 + (ANY,) * 6, matrix, limit=60,
    )
    arrived = exchange(terms, "z")
    by_k = call(merge_kernel, (block,) * 4, (place, *by_y), (ANY,) * 4, (SMEM,) + (VMEM,) * 4, sems(16), moved=3670016, limit=60)
    latter_factor = to_windows(*by_k)
    copies = call(close_kernel, f32(X * C * Y, 2 * QUAD, 16, 128), (arrived, *near, *first_factor[1:], *by_k), VMEM, (VMEM,) * 6 + (ANY,) * 7)
    rows = exchange(copies, SPREAD)

    update = call(
        update_kernel, f32(X * C * Y, 16, width), (place, rows, *first_factor, *latter_factor),
        ANY, (SMEM,) + (ANY,) * 9,
        [
            pltpu.VMEM(rows.shape, jnp.float32),
            pltpu.VMEM((2, QUAD, Y, 32, width), jnp.float32),
            pltpu.VMEM((X * C * Y, 16, width), jnp.float32),
        ] + sems(17),
        flops=2818572288, moved=7602176, limit=60,
    )
    parts = exchange(update, COLS)
    parts = parts.reshape(2, QUAD, Y, *parts.shape[1:])
    reduced = trail_rhs - (parts[0] + parts[1]).transpose(2, 1, 0, 3).reshape(trail_rhs.shape)

    own = lambda panel: lax.dynamic_slice(
        rows, (prow * Y, panel * QUAD, 0, y * narrow), (Y, 1, rows.shape[2], narrow)
    ).reshape(strip, narrow)
    solved = jnp.stack([own(0), own(1)], axis=1)
    return solved, reduced


def solution(mesh):
    devices = Mesh(mesh.devices.reshape(X, C, Z, Y), ("x", "c", "z", "y"))
    placed = (
        P(ROWS, None, COLS),
        P(None, COLS, None),
        P(COLS, None),
        P(None, COLS, ROWS),
        P(COLS, ROWS),
    )
    return jax.shard_map(
        body,
        mesh=devices,
        in_specs=placed,
        out_specs=(P(ROWS, None, COLS), P(COLS, ROWS)),
        check_vma=False,
    )
```

```python
import functools

import jax
import jax.numpy as jnp
from jax import lax
from jax.experimental import pallas as pl
from jax.experimental.pallas import tpu as pltpu
from jax.sharding import Mesh, PartitionSpec as P

X, C, Z, Y = 4, 2, 8, 4
ROWS = ("x", "c")
COLS = ("z", "y")
SPREAD = ("x", "c", "y")
QUAD = 4
NEAR = (0, -1, 1, 2, -2)
VMEM = pl.BlockSpec(memory_space=pltpu.VMEM)
ANY = pl.BlockSpec(memory_space=pl.ANY)
SMEM = pl.BlockSpec(memory_space=pltpu.SMEM)


def f32(*shape):
    return jax.ShapeDtypeStruct(shape, jnp.float32)


def call(kernel, outs, ins, out_specs, in_specs, scratch=(), flops=0, moved=0, limit=16):
    return pl.pallas_call(
        kernel,
        out_shape=outs,
        in_specs=in_specs,
        out_specs=out_specs,
        scratch_shapes=scratch,
        compiler_params=pltpu.CompilerParams(vmem_limit_bytes=limit << 20),
        cost_estimate=pl.CostEstimate(flops=flops, bytes_accessed=moved, transcendentals=0),
    )(*ins)


def exact_dot(left, right):
    return lax.dot_general(
        left, right, (((1,), (0,)), ((), ())),
        precision=lax.Precision.HIGHEST, preferred_element_type=jnp.float32,
    )


def split(value):
    high = value.astype(jnp.bfloat16)
    return high, (value - high.astype(jnp.float32)).astype(jnp.bfloat16)


def copy_all(copies, sems):
    started = [pltpu.make_async_copy(src, dst, sems.at[i]) for i, (src, dst) in enumerate(copies)]
    for copy in started:
        copy.start()
    for copy in started:
        copy.wait()


def open_kernel(rhs, inverse, terms):
    product = exact_dot(rhs[...], inverse[0])
    rows = rhs.shape[0] // Y
    for z in range(Z):
        for y in range(Y):
            terms[z * Y + y] = product[y * rows:(y + 1) * rows, z * 128:(z + 1) * 128]


def share_kernel(place, rhs, inverse, couple, *shared):
    for r in range(Y):
        rows = pl.ds(pl.multiple_of((place[1] + r) % Y * 16, 16), 16)
        piece = rhs[rows]
        shared[r][0:32] = couple[...]
        shared[r][32:64] = inverse[1]
        shared[r][64:72] = jnp.zeros((8, shared[r].shape[1]), jnp.float32)
        shared[r][64:72, 0:128] = piece[0:8]
        shared[r][64:72, 128:256] = piece[8:16]


def in_order(place, shared, rows, matrix):
    for r in range(Y):
        matrix[(place[1] + Y - r) % Y] = shared[r][rows]
    return matrix[...].reshape(Y * 32, -1)


def couple_kernel(place, arrived, *refs):
    shared, (terms, matrix) = refs[:Y], refs[-2:]
    total = jnp.sum(arrived[...], axis=0)
    product = exact_dot(total, in_order(place, shared, slice(0, 32), matrix))
    for z in range(Z):
        terms[z, 0] = product[:, z * 128:(z + 1) * 128]
        terms[z, 1] = total


def latter_kernel(place, arrived, *refs):
    shared, (terms, matrix) = refs[:Y], refs[-2:]
    rhs = sum(piece[64:72] for piece in shared)
    rhs = jnp.concatenate([rhs[:, 0:128], rhs[:, 128:256]], axis=0)
    second = rhs - jnp.sum(arrived[:, 0], axis=0)
    product = exact_dot(second, in_order(place, shared, slice(32, 64), matrix))
    part = lambda z: product[:, (z % Z) * 128:(z % Z + 1) * 128]
    for z in range(Z):
        for k, step in enumerate(NEAR):
            terms[z, k] = part(z + step)


def close_kernel(place, first, arrived, ready, copies):
    latter = jnp.sum(arrived[...], axis=0)
    near = [first[(place[0] + Z + step) % Z, 1] for step in NEAR]
    for target in range(X * C * Y):
        for k in range(QUAD):
            pick = k if k < 3 else 3 + target // Y % C
            copies[target, k] = near[pick]
            copies[target, QUAD + k] = latter[pick]


def around(z):
    return (z % QUAD, (z + 1) % QUAD, (z + 3) % QUAD, (z + 2) % QUAD)


def cut_kernel(place, factor, *refs):
    by_class, by_y, sems = refs[:4], refs[4:8], refs[8]
    classes = around(place[0])
    width = by_y[0].shape[2]
    copies = []
    for r in range(Y):
        for k in range(QUAD):
            strip = pl.multiple_of(((place[1] + r) % Y * QUAD + classes[k]) * width, width)
            copies.append((factor.at[0, :, pl.ds(strip, width)], by_class[k].at[r]))
            copies.append((factor.at[1, :, pl.ds(strip, width)], by_y[r].at[k]))
    copy_all(copies, sems)


def turn_kernel(*refs):
    arrived, sent, sems = refs[:4], refs[4:8], refs[8]
    copy_all([(arrived[k].at[r], sent[r].at[k]) for r in range(Y) for k in range(QUAD)], sems)


def merge_kernel(place, *refs):
    arrived, sent, sems = refs[:4], refs[4:8], refs[8]
    copy_all([(arrived[r].at[k], sent[k].at[(place[1] + Y - r) % Y]) for r in range(Y) for k in range(QUAD)], sems)


def update_kernel(place, rows, *refs):
    by_r, by_k = refs[:Y], refs[Y:Y + QUAD]
    out, left, factor, result, sems = refs[-5:]
    start = lambda src, dst, i: pltpu.make_async_copy(src, dst, sems.at[i])
    chunk = 128 // 16
    part = lambda i: slice(i * chunk, (i + 1) * chunk)
    arriving = [start(rows, left, 0)]
    arriving += [start(by_r[r], factor.at[0, :, (place[1] + Y - r) % Y], 1 + r) for r in range(Y)]
    arriving += [start(by_k[k], factor.at[1, k], 1 + Y + k) for k in range(QUAD)]
    for copy in arriving:
        copy.start()
    for copy in arriving:
        copy.wait()
    right_high, right_low = split(factor[...].reshape(2 * QUAD * 128, -1))
    dot = functools.partial(jnp.dot, preferred_element_type=jnp.float32)
    sent = []
    for i in range(left.shape[0] // chunk):
        piece = left[part(i)]
        high, low = split(jnp.concatenate([piece[:, k].reshape(128, 128) for k in range(2 * QUAD)], axis=1))
        product = dot(high, right_high) + (dot(high, right_low) + dot(low, right_high))
        result[part(i)] = product.reshape(chunk, 16, -1)
        sent.append(start(result.at[part(i)], out.at[part(i)], 1 + Y + QUAD + i))
        sent[-1].start()
    for copy in sent:
        copy.wait()


def shift_y(value, step):
    return lax.ppermute(value, "y", [(y, (y + step) % Y) for y in range(Y)])


def shift_z(value, step):
    return lax.ppermute(value, "z", [(z, (z + step) % Z) for z in range(Z)])


def shift_far(value):
    pairs = [
        (c * Z + z, c * Z + (z + (2 if c else -2)) % Z) for c in range(C) for z in range(Z)
    ]
    return lax.ppermute(value, ("c", "z"), pairs)


def to_windows(own, up, down, far):
    return own, shift_z(up, 1), shift_z(down, -1), shift_far(far)


def to_ys(own, *others):
    return own, *(shift_y(other, step + 1) for step, other in enumerate(others))


def exchange(value, axes):
    return lax.all_to_all(value, axes, 0, 0, tiled=True)


def body(panel_rhs, diag_inv, coupling, trail_factor, trail_rhs):
    z, y = lax.axis_index("z"), lax.axis_index("y")
    prow = lax.axis_index("x") * C + lax.axis_index("c")
    place = jnp.stack([z, y]).astype(jnp.int32)
    strip, narrow = panel_rhs.shape[0], panel_rhs.shape[2]
    width = trail_rhs.shape[1] // (QUAD * Y)
    block = f32(QUAD, 32, width)
    sems = lambda n: [pltpu.SemaphoreType.DMA((n,))]
    matrix = [pltpu.VMEM((Y, 32, 1024), jnp.float32)]

    rhs = panel_rhs.transpose(1, 0, 2)
    lanes = lax.broadcasted_iota(jnp.int32, (1, 128), 1) // narrow
    second_rhs = jnp.where(lanes == y, jnp.tile(rhs[1], (1, Y)), 0.0)
    shared = call(
        share_kernel, (f32(72, 1024),) * Y, (place, second_rhs, diag_inv, coupling),
        (VMEM,) * Y, (SMEM,) + (VMEM,) * 3,
    )
    shared = to_ys(*shared)
    terms = call(open_kernel, f32(Z * Y, 16, 128), (rhs[0], diag_inv), VMEM, (VMEM,) * 2)
    arrived = exchange(terms, COLS)

    cut = call(
        cut_kernel, (block,) * 8, (place, trail_factor), (ANY,) * 8, (SMEM, VMEM), sems(32), moved=7340032, limit=60,
    )
    by_class, by_y = to_windows(*cut[:4]), to_ys(*cut[4:])

    terms = call(
        couple_kernel, f32(Z, 2, 16, 128), (place, arrived, *shared, cut[0], cut[4]),
        VMEM, (SMEM,) + (VMEM,) * 5 + (ANY,) * 2, matrix, limit=60,
    )
    first = exchange(terms, "z")
    by_r = call(turn_kernel, (block,) * 4, by_class, (ANY,) * 4, (VMEM,) * 4, sems(16), moved=3670016, limit=60)
    first_factor = to_ys(*by_r)

    terms = call(
        latter_kernel, f32(Z, len(NEAR), 16, 128), (place, first, *shared, *by_class[1:], *by_y[1:]),
        VMEM, (SMEM,) + (VMEM,) * 5 + (ANY,) * 6, matrix, limit=60,
    )
    arrived = exchange(terms, "z")
    by_k = call(merge_kernel, (block,) * 4, (place, *by_y), (ANY,) * 4, (SMEM,) + (VMEM,) * 4, sems(16), moved=3670016, limit=60)
    latter_factor = to_windows(*by_k)
    copies = call(close_kernel, f32(X * C * Y, 2 * QUAD, 16, 128), (place, first, arrived, by_r[0]), VMEM, (SMEM, VMEM, VMEM, ANY))
    rows = exchange(copies, SPREAD)

    update = call(
        update_kernel, f32(X * C * Y, 16, width), (place, rows, *first_factor, *latter_factor),
        ANY, (SMEM,) + (ANY,) * 9,
        [
            pltpu.VMEM(rows.shape, jnp.float32),
            pltpu.VMEM((2, QUAD, Y, 32, width), jnp.float32),
            pltpu.VMEM((X * C * Y, 16, width), jnp.float32),
        ] + sems(17),
        flops=2818572288, moved=7602176, limit=60,
    )
    parts = exchange(update, COLS)
    parts = parts.reshape(2, QUAD, Y, *parts.shape[1:])
    reduced = trail_rhs - (parts[0] + parts[1]).transpose(2, 1, 0, 3).reshape(trail_rhs.shape)

    own = lambda panel: lax.dynamic_slice(
        rows, (prow * Y, panel * QUAD, 0, y * narrow), (Y, 1, rows.shape[2], narrow)
    ).reshape(strip, narrow)
    solved = jnp.stack([own(0), own(1)], axis=1)
    return solved, reduced


def solution(mesh):
    devices = Mesh(mesh.devices.reshape(X, C, Z, Y), ("x", "c", "z", "y"))
    placed = (
        P(ROWS, None, COLS),
        P(None, COLS, None),
        P(COLS, None),
        P(None, COLS, ROWS),
        P(COLS, ROWS),
    )
    return jax.shard_map(
        body,
        mesh=devices,
        in_specs=placed,
        out_specs=(P(ROWS, None, COLS), P(COLS, ROWS)),
        check_vma=False,
    )
```

```python
import functools

import jax
import jax.numpy as jnp
from jax import lax
from jax.experimental import pallas as pl
from jax.experimental.pallas import tpu as pltpu
from jax.sharding import Mesh, PartitionSpec as P

X, C, Z, Y = 4, 2, 8, 4
ROWS = ("x", "c")
COLS = ("z", "y")
SPREAD = ("x", "c", "y")
QUAD = 4
NEAR = (0, -1, 1, 2, -2)
VMEM = pl.BlockSpec(memory_space=pltpu.VMEM)
ANY = pl.BlockSpec(memory_space=pl.ANY)
SMEM = pl.BlockSpec(memory_space=pltpu.SMEM)


def f32(*shape):
    return jax.ShapeDtypeStruct(shape, jnp.float32)


def call(kernel, outs, ins, out_specs, in_specs, scratch=(), flops=0, moved=0, limit=16):
    return pl.pallas_call(
        kernel,
        out_shape=outs,
        in_specs=in_specs,
        out_specs=out_specs,
        scratch_shapes=scratch,
        compiler_params=pltpu.CompilerParams(vmem_limit_bytes=limit << 20),
        cost_estimate=pl.CostEstimate(flops=flops, bytes_accessed=moved, transcendentals=0),
    )(*ins)


def exact_dot(left, right):
    return lax.dot_general(
        left, right, (((1,), (0,)), ((), ())),
        precision=lax.Precision.HIGHEST, preferred_element_type=jnp.float32,
    )


def split(value):
    high = value.astype(jnp.bfloat16)
    return high, (value - high.astype(jnp.float32)).astype(jnp.bfloat16)


def copy_all(copies, sems):
    started = [pltpu.make_async_copy(src, dst, sems.at[i]) for i, (src, dst) in enumerate(copies)]
    for copy in started:
        copy.start()
    for copy in started:
        copy.wait()


def open_kernel(rhs, inverse, terms):
    product = exact_dot(rhs[...], inverse[0])
    rows = rhs.shape[0] // Y
    for z in range(Z):
        for y in range(Y):
            terms[z * Y + y] = product[y * rows:(y + 1) * rows, z * 128:(z + 1) * 128]


def share_kernel(place, rhs, inverse, couple, *shared):
    for r in range(Y):
        rows = pl.ds(pl.multiple_of((place[1] + r) % Y * 16, 16), 16)
        piece = rhs[rows]
        shared[r][0:32] = couple[...]
        shared[r][32:64] = inverse[1]
        shared[r][64:72] = jnp.zeros((8, shared[r].shape[1]), jnp.float32)
        shared[r][64:72, 0:128] = piece[0:8]
        shared[r][64:72, 128:256] = piece[8:16]


def in_order(place, shared, rows, matrix):
    for r in range(Y):
        matrix[(place[1] + Y - r) % Y] = shared[r][rows]
    return matrix[...].reshape(Y * 32, -1)


def couple_kernel(place, arrived, *refs):
    shared, (terms, matrix) = refs[:Y], refs[-2:]
    total = jnp.sum(arrived[...], axis=0)
    product = exact_dot(total, in_order(place, shared, slice(0, 32), matrix))
    for z in range(Z):
        terms[z, 0] = product[:, z * 128:(z + 1) * 128]
        terms[z, 1] = total


def latter_kernel(place, arrived, *refs):
    shared, (terms, matrix) = refs[:Y], refs[-2:]
    rhs = sum(piece[64:72] for piece in shared)
    rhs = jnp.concatenate([rhs[:, 0:128], rhs[:, 128:256]], axis=0)
    second = rhs - jnp.sum(arrived[:, 0], axis=0)
    product = exact_dot(second, in_order(place, shared, slice(32, 64), matrix))
    part = lambda z: product[:, (z % Z) * 128:(z % Z + 1) * 128]
    for z in range(Z):
        for k, step in enumerate(NEAR):
            terms[z, k] = part(z + step)


def close_kernel(place, first, arrived, ready, copies):
    latter = jnp.sum(arrived[...], axis=0)
    near = [first[(place[0] + Z + step) % Z, 1] for step in NEAR]
    for target in range(X * C * Y):
        for k in range(QUAD):
            pick = k if k < 3 else 3 + target // Y % C
            copies[target, k] = near[pick]
            copies[target, QUAD + k] = latter[pick]


def around(z):
    return (z % QUAD, (z + 1) % QUAD, (z + 3) % QUAD, (z + 2) % QUAD)


def cut_kernel(place, factor, *refs):
    by_class, by_y, sems = refs[:4], refs[4:8], refs[8]
    classes = around(place[0])
    width = by_y[0].shape[2]
    copies = []
    for r in range(Y):
        for k in range(QUAD):
            strip = pl.multiple_of(((place[1] + r) % Y * QUAD + classes[k]) * width, width)
            copies.append((factor.at[0, :, pl.ds(strip, width)], by_class[k].at[r]))
            copies.append((factor.at[1, :, pl.ds(strip, width)], by_y[r].at[k]))
    copy_all(copies, sems)


def turn_kernel(*refs):
    arrived, sent, sems = refs[:4], refs[4:8], refs[8]
    copy_all([(arrived[k].at[r], sent[r].at[k]) for r in range(Y) for k in range(QUAD)], sems)


def merge_kernel(place, *refs):
    arrived, sent, sems = refs[:4], refs[4:8], refs[8]
    copy_all([(arrived[r].at[k], sent[k].at[(place[1] + Y - r) % Y]) for r in range(Y) for k in range(QUAD)], sems)


def split_first_kernel(place, *refs):
    arrived, (high, low) = refs[:Y], refs[Y:]
    for r in range(Y):
        slot = (place[1] + Y - r) % Y
        high[:, slot], low[:, slot] = split(arrived[r][...])


def split_latter_kernel(*refs):
    arrived, (high, low) = refs[:QUAD], refs[QUAD:]
    for k in range(QUAD):
        high[k], low[k] = split(arrived[k][...])


def update_kernel(rows, *refs):
    parts, (out, left, factor, result, sems) = refs[:4], refs[4:]
    start = lambda src, dst, i: pltpu.make_async_copy(src, dst, sems.at[i])
    chunk = 128 // 16
    at = lambda i: slice(i * chunk, (i + 1) * chunk)
    arriving = [start(rows, left, 0)]
    arriving += [start(parts[i], factor.at[i % 2, i // 2], 1 + i) for i in range(4)]
    for copy in arriving:
        copy.start()
    for copy in arriving:
        copy.wait()
    right_high, right_low = (factor[i].reshape(2 * QUAD * 128, -1) for i in range(2))
    dot = functools.partial(jnp.dot, preferred_element_type=jnp.float32)
    sent = []
    for i in range(left.shape[0] // chunk):
        piece = left[at(i)]
        high, low = split(jnp.concatenate([piece[:, k].reshape(128, 128) for k in range(2 * QUAD)], axis=1))
        product = dot(high, right_high) + (dot(high, right_low) + dot(low, right_high))
        result[at(i)] = product.reshape(chunk, 16, -1)
        sent.append(start(result.at[at(i)], out.at[at(i)], 5 + i))
        sent[-1].start()
    for copy in sent:
        copy.wait()


def shift_y(value, step):
    return lax.ppermute(value, "y", [(y, (y + step) % Y) for y in range(Y)])


def shift_z(value, step):
    return lax.ppermute(value, "z", [(z, (z + step) % Z) for z in range(Z)])


def shift_far(value):
    pairs = [
        (c * Z + z, c * Z + (z + (2 if c else -2)) % Z) for c in range(C) for z in range(Z)
    ]
    return lax.ppermute(value, ("c", "z"), pairs)


def to_windows(own, up, down, far):
    return own, shift_z(up, 1), shift_z(down, -1), shift_far(far)


def to_ys(own, *others):
    return own, *(shift_y(other, step + 1) for step, other in enumerate(others))


def exchange(value, axes):
    return lax.all_to_all(value, axes, 0, 0, tiled=True)


def body(panel_rhs, diag_inv, coupling, trail_factor, trail_rhs):
    z, y = lax.axis_index("z"), lax.axis_index("y")
    prow = lax.axis_index("x") * C + lax.axis_index("c")
    place = jnp.stack([z, y]).astype(jnp.int32)
    strip, narrow = panel_rhs.shape[0], panel_rhs.shape[2]
    width = trail_rhs.shape[1] // (QUAD * Y)
    block = f32(QUAD, 32, width)
    sems = lambda n: [pltpu.SemaphoreType.DMA((n,))]
    matrix = [pltpu.VMEM((Y, 32, 1024), jnp.float32)]

    rhs = panel_rhs.transpose(1, 0, 2)
    lanes = lax.broadcasted_iota(jnp.int32, (1, 128), 1) // narrow
    second_rhs = jnp.where(lanes == y, jnp.tile(rhs[1], (1, Y)), 0.0)
    shared = call(
        share_kernel, (f32(72, 1024),) * Y, (place, second_rhs, diag_inv, coupling),
        (VMEM,) * Y, (SMEM,) + (VMEM,) * 3,
    )
    shared = to_ys(*shared)
    terms = call(open_kernel, f32(Z * Y, 16, 128), (rhs[0], diag_inv), VMEM, (VMEM,) * 2)
    arrived = exchange(terms, COLS)

    cut = call(
        cut_kernel, (block,) * 8, (place, trail_factor), (ANY,) * 8, (SMEM, VMEM), sems(32), moved=7340032, limit=60,
    )
    by_class, by_y = to_windows(*cut[:4]), to_ys(*cut[4:])

    terms = call(
        couple_kernel, f32(Z, 2, 16, 128), (place, arrived, *shared, cut[0], cut[4]),
        VMEM, (SMEM,) + (VMEM,) * 5 + (ANY,) * 2, matrix, limit=60,
    )
    first = exchange(terms, "z")
    by_r = call(turn_kernel, (block,) * 4, by_class, (ANY,) * 4, (VMEM,) * 4, sems(16), moved=3670016, limit=60)
    first_factor = to_ys(*by_r)

    terms = call(
        latter_kernel, f32(Z, len(NEAR), 16, 128), (place, first, *shared, *by_class[1:], *by_y[1:]),
        VMEM, (SMEM,) + (VMEM,) * 5 + (ANY,) * 6, matrix, limit=60,
    )
    arrived = exchange(terms, "z")
    by_k = call(merge_kernel, (block,) * 4, (place, *by_y), (ANY,) * 4, (SMEM,) + (VMEM,) * 4, sems(16), moved=3670016, limit=60)
    latter_factor = to_windows(*by_k)
    copies = call(close_kernel, f32(X * C * Y, 2 * QUAD, 16, 128), (place, first, arrived, by_r[0]), VMEM, (SMEM, VMEM, VMEM, ANY))
    rows = exchange(copies, SPREAD)

    halves = (jax.ShapeDtypeStruct((QUAD, *block.shape), jnp.bfloat16),) * 2
    first_parts = call(
        split_first_kernel, halves, (place, *first_factor), (VMEM,) * 2, (SMEM,) + (VMEM,) * 4, moved=100 << 20, limit=60,
    )
    latter_parts = call(
        split_latter_kernel, halves, latter_factor, (VMEM,) * 2, (VMEM,) * 4, moved=50 << 20, limit=60,
    )
    update = call(
        update_kernel, f32(X * C * Y, 16, width), (rows, *first_parts, *latter_parts), ANY, (ANY,) * 5,
        [
            pltpu.VMEM(rows.shape, jnp.float32),
            pltpu.VMEM((2, 2, QUAD, *block.shape), jnp.bfloat16),
            pltpu.VMEM((X * C * Y, 16, width), jnp.float32),
        ] + sems(9),
        flops=2818572288, moved=7602176, limit=60,
    )
    parts = exchange(update, COLS)
    parts = parts.reshape(2, QUAD, Y, *parts.shape[1:])
    reduced = trail_rhs - (parts[0] + parts[1]).transpose(2, 1, 0, 3).reshape(trail_rhs.shape)

    own = lambda panel: lax.dynamic_slice(
        rows, (prow * Y, panel * QUAD, 0, y * narrow), (Y, 1, rows.shape[2], narrow)
    ).reshape(strip, narrow)
    solved = jnp.stack([own(0), own(1)], axis=1)
    return solved, reduced


def solution(mesh):
    devices = Mesh(mesh.devices.reshape(X, C, Z, Y), ("x", "c", "z", "y"))
    placed = (
        P(ROWS, None, COLS),
        P(None, COLS, None),
        P(COLS, None),
        P(None, COLS, ROWS),
        P(COLS, ROWS),
    )
    return jax.shard_map(
        body,
        mesh=devices,
        in_specs=placed,
        out_specs=(P(ROWS, None, COLS), P(COLS, ROWS)),
        check_vma=False,
    )
```

```python
import functools

import jax
import jax.numpy as jnp
from jax import lax
from jax.experimental import pallas as pl
from jax.experimental.pallas import tpu as pltpu
from jax.sharding import Mesh, PartitionSpec as P

X, C, Z, Y = 4, 2, 8, 4
ROWS = ("x", "c")
COLS = ("z", "y")
SPREAD = ("x", "c", "y")
QUAD = 4
NEAR = (0, -1, 1, 2, -2)
VMEM = pl.BlockSpec(memory_space=pltpu.VMEM)
ANY = pl.BlockSpec(memory_space=pl.ANY)
SMEM = pl.BlockSpec(memory_space=pltpu.SMEM)


def f32(*shape):
    return jax.ShapeDtypeStruct(shape, jnp.float32)


def call(kernel, outs, ins, out_specs, in_specs, scratch=(), flops=0, moved=0, limit=16):
    return pl.pallas_call(
        kernel,
        out_shape=outs,
        in_specs=in_specs,
        out_specs=out_specs,
        scratch_shapes=scratch,
        compiler_params=pltpu.CompilerParams(vmem_limit_bytes=limit << 20),
        cost_estimate=pl.CostEstimate(flops=flops, bytes_accessed=moved, transcendentals=0),
    )(*ins)


def exact_dot(left, right):
    return lax.dot_general(
        left, right, (((1,), (0,)), ((), ())),
        precision=lax.Precision.HIGHEST, preferred_element_type=jnp.float32,
    )


def split(value):
    high = value.astype(jnp.bfloat16)
    return high, (value - high.astype(jnp.float32)).astype(jnp.bfloat16)


def copy_all(copies, sems):
    started = [pltpu.make_async_copy(src, dst, sems.at[i]) for i, (src, dst) in enumerate(copies)]
    for copy in started:
        copy.start()
    for copy in started:
        copy.wait()


def open_kernel(rhs, inverse, terms):
    product = exact_dot(rhs[...], inverse[0])
    rows = rhs.shape[0] // Y
    for z in range(Z):
        for y in range(Y):
            terms[z * Y + y] = product[y * rows:(y + 1) * rows, z * 128:(z + 1) * 128]


def share_kernel(place, rhs, inverse, couple, *shared):
    for r in range(Y):
        rows = pl.ds(pl.multiple_of((place[1] + r) % Y * 16, 16), 16)
        piece = rhs[rows]
        shared[r][0:32] = couple[...]
        shared[r][32:64] = inverse[1]
        shared[r][64:72] = jnp.zeros((8, shared[r].shape[1]), jnp.float32)
        shared[r][64:72, 0:128] = piece[0:8]
        shared[r][64:72, 128:256] = piece[8:16]


def in_order(place, shared, rows, matrix):
    for r in range(Y):
        matrix[(place[1] + Y - r) % Y] = shared[r][rows]
    return matrix[...].reshape(Y * 32, -1)


def couple_kernel(place, arrived, *refs):
    shared, (terms, matrix) = refs[:Y], refs[-2:]
    total = jnp.sum(arrived[...], axis=0)
    product = exact_dot(total, in_order(place, shared, slice(0, 32), matrix))
    for z in range(Z):
        terms[z, 0] = product[:, z * 128:(z + 1) * 128]
        terms[z, 1] = total


def latter_kernel(place, arrived, *refs):
    shared, (terms, matrix) = refs[:Y], refs[-2:]
    rhs = sum(piece[64:72] for piece in shared)
    rhs = jnp.concatenate([rhs[:, 0:128], rhs[:, 128:256]], axis=0)
    second = rhs - jnp.sum(arrived[:, 0], axis=0)
    product = exact_dot(second, in_order(place, shared, slice(32, 64), matrix))
    part = lambda z: product[:, (z % Z) * 128:(z % Z + 1) * 128]
    for z in range(Z):
        for k, step in enumerate(NEAR):
            terms[z, k] = part(z + step)


def close_kernel(place, first, arrived, *refs):
    copies = refs[-1]
    latter = jnp.sum(arrived[...], axis=0)
    near = [first[(place[0] + Z + step) % Z, 1] for step in NEAR]
    for target in range(X * C * Y):
        for k in range(QUAD):
            pick = k if k < 3 else 3 + target // Y % C
            copies[target, k] = near[pick]
            copies[target, QUAD + k] = latter[pick]


def around(z):
    return (z % QUAD, (z + 1) % QUAD, (z + 3) % QUAD, (z + 2) % QUAD)


def cut_kernel(place, factor, *refs):
    by_class, by_y, sems = refs[:4], refs[4:8], refs[8]
    classes = around(place[0])
    width = by_y[0].shape[2]
    copies = []
    for r in range(Y):
        for k in range(QUAD):
            strip = pl.multiple_of(((place[1] + r) % Y * QUAD + classes[k]) * width, width)
            copies.append((factor.at[0, :, pl.ds(strip, width)], by_class[k].at[r]))
            copies.append((factor.at[1, :, pl.ds(strip, width)], by_y[r].at[k]))
    copy_all(copies, sems)


def turn_kernel(*refs):
    arrived, sent, sems = refs[:4], refs[4:8], refs[8]
    copy_all([(arrived[k].at[r], sent[r].at[k]) for r in range(Y) for k in range(QUAD)], sems)


def merge_kernel(place, *refs):
    arrived, sent, sems = refs[:4], refs[4:8], refs[8]
    copy_all([(arrived[r].at[k], sent[k].at[(place[1] + Y - r) % Y]) for r in range(Y) for k in range(QUAD)], sems)


def update_kernel(place, rows, *refs):
    by_r, by_k = refs[:Y], refs[Y:Y + QUAD]
    out, left, factor, result, sems = refs[-5:]
    start = lambda src, dst, i: pltpu.make_async_copy(src, dst, sems.at[i])
    chunk = 128 // 16
    part = lambda i: slice(i * chunk, (i + 1) * chunk)
    arriving = [start(rows, left, 0)]
    arriving += [start(by_r[r], factor.at[0, :, (place[1] + Y - r) % Y], 1 + r) for r in range(Y)]
    arriving += [start(by_k[k], factor.at[1, k], 1 + Y + k) for k in range(QUAD)]
    for copy in arriving:
        copy.start()
    for copy in arriving:
        copy.wait()
    right_high, right_low = split(factor[...].reshape(2 * QUAD * 128, -1))
    dot = functools.partial(jnp.dot, preferred_element_type=jnp.float32)
    sent = []
    for i in range(left.shape[0] // chunk):
        piece = left[part(i)]
        high, low = split(jnp.concatenate([piece[:, k].reshape(128, 128) for k in range(2 * QUAD)], axis=1))
        product = dot(high, right_high) + (dot(high, right_low) + dot(low, right_high))
        result[part(i)] = product.reshape(chunk, 16, -1)
        sent.append(start(result.at[part(i)], out.at[part(i)], 1 + Y + QUAD + i))
        sent[-1].start()
    for copy in sent:
        copy.wait()


def shift_y(value, step):
    return lax.ppermute(value, "y", [(y, (y + step) % Y) for y in range(Y)])


def shift_z(value, step):
    return lax.ppermute(value, "z", [(z, (z + step) % Z) for z in range(Z)])


def shift_far(value):
    pairs = [
        (c * Z + z, c * Z + (z + (2 if c else -2)) % Z) for c in range(C) for z in range(Z)
    ]
    return lax.ppermute(value, ("c", "z"), pairs)


def to_windows(own, up, down, far):
    return own, shift_z(up, 1), shift_z(down, -1), shift_far(far)


def to_ys(own, *others):
    return own, *(shift_y(other, step + 1) for step, other in enumerate(others))


def exchange(value, axes):
    return lax.all_to_all(value, axes, 0, 0, tiled=True)


def body(panel_rhs, diag_inv, coupling, trail_factor, trail_rhs):
    z, y = lax.axis_index("z"), lax.axis_index("y")
    prow = lax.axis_index("x") * C + lax.axis_index("c")
    place = jnp.stack([z, y]).astype(jnp.int32)
    strip, narrow = panel_rhs.shape[0], panel_rhs.shape[2]
    width = trail_rhs.shape[1] // (QUAD * Y)
    block = f32(QUAD, 32, width)
    sems = lambda n: [pltpu.SemaphoreType.DMA((n,))]
    matrix = [pltpu.VMEM((Y, 32, 1024), jnp.float32)]

    rhs = panel_rhs.transpose(1, 0, 2)
    lanes = lax.broadcasted_iota(jnp.int32, (1, 128), 1) // narrow
    second_rhs = jnp.where(lanes == y, jnp.tile(rhs[1], (1, Y)), 0.0)
    shared = call(
        share_kernel, (f32(72, 1024),) * Y, (place, second_rhs, diag_inv, coupling),
        (VMEM,) * Y, (SMEM,) + (VMEM,) * 3,
    )
    shared = to_ys(*shared)
    terms = call(open_kernel, f32(Z * Y, 16, 128), (rhs[0], diag_inv), VMEM, (VMEM,) * 2)
    arrived = exchange(terms, COLS)

    cut = call(
        cut_kernel, (block,) * 8, (place, trail_factor), (ANY,) * 8, (SMEM, VMEM), sems(32), moved=7340032, limit=60,
    )
    by_class, by_y = to_windows(*cut[:4]), to_ys(*cut[4:])

    terms = call(
        couple_kernel, f32(Z, 2, 16, 128), (place, arrived, *shared, cut[0], cut[4]),
        VMEM, (SMEM,) + (VMEM,) * 5 + (ANY,) * 2, matrix, limit=60,
    )
    first = exchange(terms, "z")
    by_r = call(turn_kernel, (block,) * 4, by_class, (ANY,) * 4, (VMEM,) * 4, sems(16), moved=3670016, limit=60)
    first_factor = to_ys(*by_r)

    terms = call(
        latter_kernel, f32(Z, len(NEAR), 16, 128), (place, first, *shared, *by_class[1:], *by_y[1:]),
        VMEM, (SMEM,) + (VMEM,) * 5 + (ANY,) * 6, matrix, limit=60,
    )
    arrived = exchange(terms, "z")
    by_k = call(merge_kernel, (block,) * 4, (place, *by_y), (ANY,) * 4, (SMEM,) + (VMEM,) * 4, sems(16), moved=3670016, limit=60)
    latter_factor = to_windows(*by_k)
    copies = call(close_kernel, f32(X * C * Y, 2 * QUAD, 16, 128), (place, first, arrived, first_factor[1], first_factor[3]), VMEM, (SMEM, VMEM, VMEM, ANY, ANY))
    rows = exchange(copies, SPREAD)

    update = call(
        update_kernel, f32(X * C * Y, 16, width), (place, rows, *first_factor, *latter_factor),
        ANY, (SMEM,) + (ANY,) * 9,
        [
            pltpu.VMEM(rows.shape, jnp.float32),
            pltpu.VMEM((2, QUAD, Y, 32, width), jnp.float32),
            pltpu.VMEM((X * C * Y, 16, width), jnp.float32),
        ] + sems(17),
        flops=2818572288, moved=7602176, limit=60,
    )
    parts = exchange(update, COLS)
    parts = parts.reshape(2, QUAD, Y, *parts.shape[1:])
    reduced = trail_rhs - (parts[0] + parts[1]).transpose(2, 1, 0, 3).reshape(trail_rhs.shape)

    own = lambda panel: lax.dynamic_slice(
        rows, (prow * Y, panel * QUAD, 0, y * narrow), (Y, 1, rows.shape[2], narrow)
    ).reshape(strip, narrow)
    solved = jnp.stack([own(0), own(1)], axis=1)
    return solved, reduced


def solution(mesh):
    devices = Mesh(mesh.devices.reshape(X, C, Z, Y), ("x", "c", "z", "y"))
    placed = (
        P(ROWS, None, COLS),
        P(None, COLS, None),
        P(COLS, None),
        P(None, COLS, ROWS),
        P(COLS, ROWS),
    )
    return jax.shard_map(
        body,
        mesh=devices,
        in_specs=placed,
        out_specs=(P(ROWS, None, COLS), P(COLS, ROWS)),
        check_vma=False,
    )
```

```python
import functools

import jax
import jax.numpy as jnp
from jax import lax
from jax.experimental import pallas as pl
from jax.experimental.pallas import tpu as pltpu
from jax.sharding import Mesh, PartitionSpec as P

X, C, Z, Y = 4, 2, 8, 4
ROWS = ("x", "c")
COLS = ("z", "y")
SPREAD = ("x", "c", "y")
QUAD = 4
NEAR = (0, -1, 1, 2, -2)
VMEM = pl.BlockSpec(memory_space=pltpu.VMEM)
ANY = pl.BlockSpec(memory_space=pl.ANY)
SMEM = pl.BlockSpec(memory_space=pltpu.SMEM)


def f32(*shape):
    return jax.ShapeDtypeStruct(shape, jnp.float32)


def call(kernel, outs, ins, out_specs, in_specs, scratch=(), flops=0, moved=0, limit=16):
    return pl.pallas_call(
        kernel,
        out_shape=outs,
        in_specs=in_specs,
        out_specs=out_specs,
        scratch_shapes=scratch,
        compiler_params=pltpu.CompilerParams(vmem_limit_bytes=limit << 20),
        cost_estimate=pl.CostEstimate(flops=flops, bytes_accessed=moved, transcendentals=0),
    )(*ins)


def exact_dot(left, right):
    return lax.dot_general(
        left, right, (((1,), (0,)), ((), ())),
        precision=lax.Precision.HIGHEST, preferred_element_type=jnp.float32,
    )


def split(value):
    high = value.astype(jnp.bfloat16)
    return high, (value - high.astype(jnp.float32)).astype(jnp.bfloat16)


def copy_all(copies, sems):
    started = [pltpu.make_async_copy(src, dst, sems.at[i]) for i, (src, dst) in enumerate(copies)]
    for copy in started:
        copy.start()
    for copy in started:
        copy.wait()


def open_kernel(rhs, inverse, terms):
    product = exact_dot(rhs[...], inverse[0])
    rows = rhs.shape[0] // Y
    for z in range(Z):
        for y in range(Y):
            terms[z * Y + y] = product[y * rows:(y + 1) * rows, z * 128:(z + 1) * 128]


def share_kernel(place, rhs, inverse, couple, ready, *shared):
    for r in range(Y):
        rows = pl.ds(pl.multiple_of((place[1] + r) % Y * 16, 16), 16)
        piece = rhs[rows]
        shared[r][0:32] = couple[...]
        shared[r][32:64] = inverse[1]
        shared[r][64:72] = jnp.zeros((8, shared[r].shape[1]), jnp.float32)
        shared[r][64:72, 0:128] = piece[0:8]
        shared[r][64:72, 128:256] = piece[8:16]


def in_order(place, shared, rows, matrix):
    for r in range(Y):
        matrix[(place[1] + Y - r) % Y] = shared[r][rows]
    return matrix[...].reshape(Y * 32, -1)


def couple_kernel(place, arrived, *refs):
    shared, (terms, matrix) = refs[:Y], refs[-2:]
    total = jnp.sum(arrived[...], axis=0)
    product = exact_dot(total, in_order(place, shared, slice(0, 32), matrix))
    for z in range(Z):
        terms[z, 0] = product[:, z * 128:(z + 1) * 128]
        terms[z, 1] = total


def latter_kernel(place, arrived, *refs):
    shared, (terms, matrix) = refs[:Y], refs[-2:]
    rhs = sum(piece[64:72] for piece in shared)
    rhs = jnp.concatenate([rhs[:, 0:128], rhs[:, 128:256]], axis=0)
    second = rhs - jnp.sum(arrived[:, 0], axis=0)
    product = exact_dot(second, in_order(place, shared, slice(32, 64), matrix))
    part = lambda z: product[:, (z % Z) * 128:(z % Z + 1) * 128]
    for z in range(Z):
        for k, step in enumerate(NEAR):
            terms[z, k] = part(z + step)


def close_kernel(place, first, arrived, *refs):
    copies = refs[-1]
    latter = jnp.sum(arrived[...], axis=0)
    near = [first[(place[0] + Z + step) % Z, 1] for step in NEAR]
    for target in range(X * C * Y):
        for k in range(QUAD):
            pick = k if k < 3 else 3 + target // Y % C
            copies[target, k] = near[pick]
            copies[target, QUAD + k] = latter[pick]


def around(z):
    return (z % QUAD, (z + 1) % QUAD, (z + 3) % QUAD, (z + 2) % QUAD)


def cut_kernel(place, factor, ready, *refs):
    by_class, by_y, sems = refs[:4], refs[4:8], refs[8]
    classes = around(place[0])
    width = by_y[0].shape[2]
    copies = []
    for r in range(Y):
        for k in range(QUAD):
            strip = pl.multiple_of((classes[k] * Y + (place[1] + r) % Y) * width, width)
            copies.append((factor.at[0, :, pl.ds(strip, width)], by_class[k].at[r]))
            copies.append((factor.at[1, :, pl.ds(strip, width)], by_y[r].at[k]))
    copy_all(copies, sems)


def turn_kernel(*refs):
    arrived, sent, sems = refs[:4], refs[4:8], refs[8]
    copy_all([(arrived[k].at[r], sent[r].at[k]) for r in range(Y) for k in range(QUAD)], sems)


def merge_kernel(place, *refs):
    arrived, sent, sems = refs[:4], refs[4:8], refs[8]
    copy_all([(arrived[r].at[k], sent[k].at[(place[1] + Y - r) % Y]) for r in range(Y) for k in range(QUAD)], sems)


def update_kernel(place, rows, *refs):
    by_r, by_k = refs[:Y], refs[Y:Y + QUAD]
    out, left, factor, result, sems = refs[-5:]
    start = lambda src, dst, i: pltpu.make_async_copy(src, dst, sems.at[i])
    arriving = [start(rows, left, 0)]
    arriving += [start(by_r[r], factor.at[0, :, (place[1] + Y - r) % Y], 1 + r) for r in range(Y)]
    arriving += [start(by_k[k], factor.at[1, k], 1 + Y + k) for k in range(QUAD)]
    for copy in arriving:
        copy.start()
    for copy in arriving:
        copy.wait()
    high, low = split(jnp.concatenate([left[:, k].reshape(-1, 128) for k in range(2 * QUAD)], axis=1))
    dot = functools.partial(jnp.dot, preferred_element_type=jnp.float32)
    width = factor.shape[-1]
    sent = []
    for i, begin in enumerate(range(0, width, 256)):
        at = slice(begin, min(begin + 256, width))
        right_high, right_low = split(factor[..., at].reshape(2 * QUAD * 128, -1))
        product = dot(high, right_high) + (dot(high, right_low) + dot(low, right_high))
        result[..., at] = product.reshape(left.shape[0], 16, -1)
        sent.append(start(result.at[..., at], out.at[..., at], 1 + Y + QUAD + i))
        sent[-1].start()
    for copy in sent:
        copy.wait()


def shift_y(value, step):
    return lax.ppermute(value, "y", [(y, (y + step) % Y) for y in range(Y)])


def shift_z(value, step):
    return lax.ppermute(value, "z", [(z, (z + step) % Z) for z in range(Z)])


def shift_far(value):
    pairs = [
        (c * Z + z, c * Z + (z + (2 if c else -2)) % Z) for c in range(C) for z in range(Z)
    ]
    return lax.ppermute(value, ("c", "z"), pairs)


def to_windows(own, up, down, far):
    return own, shift_z(up, 1), shift_z(down, -1), shift_far(far)


def to_ys(own, *others):
    return own, *(shift_y(other, step + 1) for step, other in enumerate(others))


def exchange(value, axes):
    return lax.all_to_all(value, axes, 0, 0, tiled=True)


def body(panel_rhs, diag_inv, coupling, trail_factor, trail_rhs):
    z, y = lax.axis_index("z"), lax.axis_index("y")
    prow = lax.axis_index("x") * C + lax.axis_index("c")
    place = jnp.stack([z, y]).astype(jnp.int32)
    strip, narrow = panel_rhs.shape[0], panel_rhs.shape[2]
    width = trail_rhs.shape[1] // (QUAD * Y)
    block = f32(QUAD, 32, width)
    sems = lambda n: [pltpu.SemaphoreType.DMA((n,))]
    matrix = [pltpu.VMEM((Y, 32, 1024), jnp.float32)]

    rhs = panel_rhs.transpose(1, 0, 2)
    lanes = lax.broadcasted_iota(jnp.int32, (1, 128), 1) // narrow
    second_rhs = jnp.where(lanes == y, jnp.tile(rhs[1], (1, Y)), 0.0)
    terms = call(open_kernel, f32(Z * Y, 16, 128), (rhs[0], diag_inv), VMEM, (VMEM,) * 2)
    arrived = exchange(terms, COLS)
    shared = call(
        share_kernel, (f32(72, 1024),) * Y, (place, second_rhs, diag_inv, coupling, terms),
        (VMEM,) * Y, (SMEM,) + (VMEM,) * 3 + (ANY,),
    )
    shared = to_ys(*shared)

    cut = call(
        cut_kernel, (block,) * 8, (place, trail_factor, terms), (ANY,) * 8, (SMEM, VMEM, ANY), sems(32), moved=7340032, limit=60,
    )
    by_class, by_y = to_windows(*cut[:4]), to_ys(*cut[4:])

    terms = call(
        couple_kernel, f32(Z, 2, 16, 128), (place, arrived, *shared, cut[0], cut[4]),
        VMEM, (SMEM,) + (VMEM,) * 5 + (ANY,) * 2, matrix, limit=60,
    )
    first = exchange(terms, "z")
    by_r = call(turn_kernel, (block,) * 4, by_class, (ANY,) * 4, (VMEM,) * 4, sems(16), moved=3670016, limit=60)
    first_factor = to_ys(*by_r)

    terms = call(
        latter_kernel, f32(Z, len(NEAR), 16, 128), (place, first, *shared, *by_class[1:], *by_y[1:]),
        VMEM, (SMEM,) + (VMEM,) * 5 + (ANY,) * 6, matrix, limit=60,
    )
    arrived = exchange(terms, "z")
    by_k = call(merge_kernel, (block,) * 4, (place, *by_y), (ANY,) * 4, (SMEM,) + (VMEM,) * 4, sems(16), moved=3670016, limit=60)
    latter_factor = to_windows(*by_k)
    copies = call(close_kernel, f32(X * C * Y, 2 * QUAD, 16, 128), (place, first, arrived, first_factor[1], first_factor[3]), VMEM, (SMEM, VMEM, VMEM, ANY, ANY))
    rows = exchange(copies, SPREAD)

    update = call(
        update_kernel, f32(X * C * Y, 16, width), (place, rows, *first_factor, *latter_factor),
        ANY, (SMEM,) + (ANY,) * 9,
        [
            pltpu.VMEM(rows.shape, jnp.float32),
            pltpu.VMEM((2, QUAD, Y, 32, width), jnp.float32),
            pltpu.VMEM((X * C * Y, 16, width), jnp.float32),
        ] + sems(17),
        flops=2818572288, moved=7602176, limit=60,
    )
    parts = exchange(update, COLS)
    parts = parts.reshape(2, QUAD * Y, *parts.shape[1:])
    reduced = trail_rhs - (parts[0] + parts[1]).transpose(1, 0, 2).reshape(trail_rhs.shape)

    own = lambda panel: lax.dynamic_slice(
        rows, (prow * Y, panel * QUAD, 0, y * narrow), (Y, 1, rows.shape[2], narrow)
    ).reshape(strip, narrow)
    solved = jnp.stack([own(0), own(1)], axis=1)
    return solved, reduced


def solution(mesh):
    devices = Mesh(mesh.devices.reshape(X, C, Z, Y), ("x", "c", "z", "y"))
    placed = (
        P(ROWS, None, COLS),
        P(None, COLS, None),
        P(COLS, None),
        P(None, COLS, ROWS),
        P(COLS, ROWS),
    )
    return jax.shard_map(
        body,
        mesh=devices,
        in_specs=placed,
        out_specs=(P(ROWS, None, COLS), P(COLS, ROWS)),
        check_vma=False,
    )
```

```python
import functools

import jax
import jax.numpy as jnp
from jax import lax
from jax.experimental import pallas as pl
from jax.experimental.pallas import tpu as pltpu
from jax.sharding import Mesh, PartitionSpec as P

X, C, Z, Y = 4, 2, 8, 4
ROWS = ("x", "c")
COLS = ("z", "y")
SPREAD = ("x", "c", "y")
QUAD = 4
NEAR = (0, -1, 1, 2, -2)
VMEM = pl.BlockSpec(memory_space=pltpu.VMEM)
ANY = pl.BlockSpec(memory_space=pl.ANY)
SMEM = pl.BlockSpec(memory_space=pltpu.SMEM)


def f32(*shape):
    return jax.ShapeDtypeStruct(shape, jnp.float32)


def call(kernel, outs, ins, out_specs, in_specs, scratch=(), flops=0, moved=0, limit=16):
    return pl.pallas_call(
        kernel,
        out_shape=outs,
        in_specs=in_specs,
        out_specs=out_specs,
        scratch_shapes=scratch,
        compiler_params=pltpu.CompilerParams(vmem_limit_bytes=limit << 20),
        cost_estimate=pl.CostEstimate(flops=flops, bytes_accessed=moved, transcendentals=0),
    )(*ins)


def exact_dot(left, right):
    return lax.dot_general(
        left, right, (((1,), (0,)), ((), ())),
        precision=lax.Precision.HIGHEST, preferred_element_type=jnp.float32,
    )


def split(value):
    high = value.astype(jnp.bfloat16)
    return high, (value - high.astype(jnp.float32)).astype(jnp.bfloat16)


def copy_all(copies, sems):
    started = [pltpu.make_async_copy(src, dst, sems.at[i]) for i, (src, dst) in enumerate(copies)]
    for copy in started:
        copy.start()
    for copy in started:
        copy.wait()


def open_kernel(rhs, inverse, terms):
    product = exact_dot(rhs[...], inverse[0])
    rows = rhs.shape[0] // Y
    for z in range(Z):
        for y in range(Y):
            terms[z * Y + y] = product[y * rows:(y + 1) * rows, z * 128:(z + 1) * 128]


def share_kernel(place, rhs, inverse, couple, *shared):
    for r in range(Y):
        rows = pl.ds(pl.multiple_of((place[1] + r) % Y * 16, 16), 16)
        piece = rhs[rows]
        shared[r][0:32] = couple[...]
        shared[r][32:64] = inverse[1]
        shared[r][64:72] = jnp.zeros((8, shared[r].shape[1]), jnp.float32)
        shared[r][64:72, 0:128] = piece[0:8]
        shared[r][64:72, 128:256] = piece[8:16]


def in_order(place, shared, rows, matrix):
    for r in range(Y):
        matrix[(place[1] + Y - r) % Y] = shared[r][rows]
    return matrix[...].reshape(Y * 32, -1)


def couple_kernel(place, arrived, *refs):
    shared, (terms, matrix) = refs[:Y], refs[-2:]
    total = jnp.sum(arrived[...], axis=0)
    product = exact_dot(total, in_order(place, shared, slice(0, 32), matrix))
    for z in range(Z):
        terms[z, 0] = product[:, z * 128:(z + 1) * 128]
        terms[z, 1] = total


def latter_kernel(place, arrived, *refs):
    shared, (terms, matrix) = refs[:Y], refs[-2:]
    rhs = sum(piece[64:72] for piece in shared)
    rhs = jnp.concatenate([rhs[:, 0:128], rhs[:, 128:256]], axis=0)
    second = rhs - jnp.sum(arrived[:, 0], axis=0)
    product = exact_dot(second, in_order(place, shared, slice(32, 64), matrix))
    part = lambda z: product[:, (z % Z) * 128:(z % Z + 1) * 128]
    for z in range(Z):
        for k, step in enumerate(NEAR):
            terms[z, k] = part(z + step)


def close_kernel(place, first, arrived, *refs):
    copies = refs[-1]
    latter = jnp.sum(arrived[...], axis=0)
    near = [first[(place[0] + Z + step) % Z, 1] for step in NEAR]
    for target in range(X * C * Y):
        for k in range(QUAD):
            pick = k if k < 3 else 3 + target // Y % C
            copies[target, k] = near[pick]
            copies[target, QUAD + k] = latter[pick]


def around(z):
    return (z % QUAD, (z + 1) % QUAD, (z + 3) % QUAD, (z + 2) % QUAD)


def cut_kernel(place, factor, ready, *refs):
    by_class, by_y, sems = refs[:4], refs[4:8], refs[8]
    classes = around(place[0])
    width = by_y[0].shape[2]
    copies = []
    for r in range(Y):
        for k in range(QUAD):
            strip = pl.multiple_of((classes[k] * Y + (place[1] + r) % Y) * width, width)
            copies.append((factor.at[0, :, pl.ds(strip, width)], by_class[k].at[r]))
            copies.append((factor.at[1, :, pl.ds(strip, width)], by_y[r].at[k]))
    copy_all(copies, sems)


def turn_kernel(*refs):
    arrived, sent, sems = refs[:4], refs[4:8], refs[8]
    copy_all([(arrived[k].at[r], sent[r].at[k]) for r in range(Y) for k in range(QUAD)], sems)


def merge_kernel(place, *refs):
    arrived, sent, sems = refs[:4], refs[4:8], refs[8]
    copy_all([(arrived[r].at[k], sent[k].at[(place[1] + Y - r) % Y]) for r in range(Y) for k in range(QUAD)], sems)


def update_kernel(place, rows, *refs):
    by_r, by_k = refs[:Y], refs[Y:Y + QUAD]
    out, high, low, result, sems = refs[Y + QUAD:]
    for r in range(Y):
        slot = (place[1] + Y - r) % Y
        high[0, :, slot], low[0, :, slot] = split(by_r[r][...])
    for k in range(QUAD):
        high[1, k], low[1, k] = split(by_k[k][...])
    left_high, left_low = split(jnp.concatenate([rows[:, k].reshape(-1, 128) for k in range(2 * QUAD)], axis=1))
    dot = functools.partial(jnp.dot, preferred_element_type=jnp.float32)
    width = result.shape[2]
    sent = []
    for i, begin in enumerate(range(0, width, 256)):
        at = slice(begin, min(begin + 256, width))
        right_high, right_low = (part[..., at].reshape(2 * QUAD * 128, -1) for part in (high, low))
        product = dot(left_high, right_high) + (dot(left_high, right_low) + dot(left_low, right_high))
        result[..., at] = product.reshape(result.shape[0], 16, -1)
        sent.append(pltpu.make_async_copy(result.at[..., at], out.at[..., at], sems.at[i]))
        sent[-1].start()
    for copy in sent:
        copy.wait()


def shift_y(value, step):
    return lax.ppermute(value, "y", [(y, (y + step) % Y) for y in range(Y)])


def shift_z(value, step):
    return lax.ppermute(value, "z", [(z, (z + step) % Z) for z in range(Z)])


def shift_far(value):
    pairs = [
        (c * Z + z, c * Z + (z + (2 if c else -2)) % Z) for c in range(C) for z in range(Z)
    ]
    return lax.ppermute(value, ("c", "z"), pairs)


def to_windows(own, up, down, far):
    return own, shift_z(up, 1), shift_z(down, -1), shift_far(far)


def to_ys(own, *others):
    return own, *(shift_y(other, step + 1) for step, other in enumerate(others))


def exchange(value, axes):
    return lax.all_to_all(value, axes, 0, 0, tiled=True)


def body(panel_rhs, diag_inv, coupling, trail_factor, trail_rhs):
    z, y = lax.axis_index("z"), lax.axis_index("y")
    prow = lax.axis_index("x") * C + lax.axis_index("c")
    place = jnp.stack([z, y]).astype(jnp.int32)
    strip, narrow = panel_rhs.shape[0], panel_rhs.shape[2]
    width = trail_rhs.shape[1] // (QUAD * Y)
    block = f32(QUAD, 32, width)
    sems = lambda n: [pltpu.SemaphoreType.DMA((n,))]
    matrix = [pltpu.VMEM((Y, 32, 1024), jnp.float32)]

    rhs = panel_rhs.transpose(1, 0, 2)
    lanes = lax.broadcasted_iota(jnp.int32, (1, 128), 1) // narrow
    second_rhs = jnp.where(lanes == y, jnp.tile(rhs[1], (1, Y)), 0.0)
    terms = call(open_kernel, f32(Z * Y, 16, 128), (rhs[0], diag_inv), VMEM, (VMEM,) * 2)
    arrived = exchange(terms, COLS)
    shared = call(
        share_kernel, (f32(72, 1024),) * Y, (place, second_rhs, diag_inv, coupling),
        (VMEM,) * Y, (SMEM,) + (VMEM,) * 3,
    )
    shared = to_ys(*shared)

    cut = call(
        cut_kernel, (block,) * 8, (place, trail_factor, shared[1]), (ANY,) * 8, (SMEM, VMEM, ANY), sems(32), moved=7340032, limit=60,
    )
    by_class, by_y = to_windows(*cut[:4]), to_ys(*cut[4:])

    terms = call(
        couple_kernel, f32(Z, 2, 16, 128), (place, arrived, *shared, cut[0], cut[4]),
        VMEM, (SMEM,) + (VMEM,) * 5 + (ANY,) * 2, matrix, limit=60,
    )
    first = exchange(terms, "z")
    by_r = call(turn_kernel, (block,) * 4, by_class, (ANY,) * 4, (VMEM,) * 4, sems(16), moved=3670016, limit=60)
    first_factor = to_ys(*by_r)

    terms = call(
        latter_kernel, f32(Z, len(NEAR), 16, 128), (place, first, *shared, *by_class[1:], *by_y[1:]),
        VMEM, (SMEM,) + (VMEM,) * 5 + (ANY,) * 6, matrix, limit=60,
    )
    arrived = exchange(terms, "z")
    by_k = call(merge_kernel, (block,) * 4, (place, *by_y), (ANY,) * 4, (SMEM,) + (VMEM,) * 4, sems(16), moved=3670016, limit=60)
    latter_factor = to_windows(*by_k)
    copies = call(close_kernel, f32(X * C * Y, 2 * QUAD, 16, 128), (place, first, arrived, first_factor[1], first_factor[3]), VMEM, (SMEM, VMEM, VMEM, ANY, ANY))
    rows = exchange(copies, SPREAD)

    part = pltpu.VMEM((2, QUAD, *block.shape), jnp.bfloat16)
    update = call(
        update_kernel, f32(X * C * Y, 16, width), (place, rows, *first_factor, *latter_factor),
        ANY, (SMEM,) + (VMEM,) * 9, [part, part, pltpu.VMEM((X * C * Y, 16, width), jnp.float32)] + sems(4),
        flops=2818572288, moved=7602176, limit=24,
    )
    parts = exchange(update, COLS)
    parts = parts.reshape(2, QUAD * Y, *parts.shape[1:])
    reduced = trail_rhs - (parts[0] + parts[1]).transpose(1, 0, 2).reshape(trail_rhs.shape)

    own = lambda panel: lax.dynamic_slice(
        rows, (prow * Y, panel * QUAD, 0, y * narrow), (Y, 1, rows.shape[2], narrow)
    ).reshape(strip, narrow)
    solved = jnp.stack([own(0), own(1)], axis=1)
    return solved, reduced


def solution(mesh):
    devices = Mesh(mesh.devices.reshape(X, C, Z, Y), ("x", "c", "z", "y"))
    placed = (
        P(ROWS, None, COLS),
        P(None, COLS, None),
        P(COLS, None),
        P(None, COLS, ROWS),
        P(COLS, ROWS),
    )
    return jax.shard_map(
        body,
        mesh=devices,
        in_specs=placed,
        out_specs=(P(ROWS, None, COLS), P(COLS, ROWS)),
        check_vma=False,
    )
```

```python
import functools

import jax
import jax.numpy as jnp
from jax import lax
from jax.experimental import pallas as pl
from jax.experimental.pallas import tpu as pltpu
from jax.sharding import Mesh, PartitionSpec as P

X, C, Z, Y = 4, 2, 8, 4
ROWS = ("x", "c")
COLS = ("z", "y")
SPREAD = ("x", "c", "y")
QUAD = 4
NEAR = (0, -1, 1, 2, -2)
VMEM = pl.BlockSpec(memory_space=pltpu.VMEM)
ANY = pl.BlockSpec(memory_space=pl.ANY)
SMEM = pl.BlockSpec(memory_space=pltpu.SMEM)


def f32(*shape):
    return jax.ShapeDtypeStruct(shape, jnp.float32)


def call(kernel, outs, ins, out_specs, in_specs, scratch=(), flops=0, moved=0, limit=16):
    return pl.pallas_call(
        kernel,
        out_shape=outs,
        in_specs=in_specs,
        out_specs=out_specs,
        scratch_shapes=scratch,
        compiler_params=pltpu.CompilerParams(vmem_limit_bytes=limit << 20),
        cost_estimate=pl.CostEstimate(flops=flops, bytes_accessed=moved, transcendentals=0),
    )(*ins)


def exact_dot(left, right):
    return lax.dot_general(
        left, right, (((1,), (0,)), ((), ())),
        precision=lax.Precision.HIGHEST, preferred_element_type=jnp.float32,
    )


def split(value):
    high = value.astype(jnp.bfloat16)
    return high, (value - high.astype(jnp.float32)).astype(jnp.bfloat16)


def copy_all(copies, sems):
    started = [pltpu.make_async_copy(src, dst, sems.at[i]) for i, (src, dst) in enumerate(copies)]
    for copy in started:
        copy.start()
    for copy in started:
        copy.wait()


def open_kernel(rhs, inverse, terms):
    product = exact_dot(rhs[...], inverse[0])
    rows = rhs.shape[0] // Y
    for z in range(Z):
        for y in range(Y):
            terms[z * Y + y] = product[y * rows:(y + 1) * rows, z * 128:(z + 1) * 128]


def share_kernel(place, rhs, inverse, couple, *shared):
    for r in range(Y):
        rows = pl.ds(pl.multiple_of((place[1] + r) % Y * 16, 16), 16)
        piece = rhs[rows]
        shared[r][0:32] = couple[...]
        shared[r][32:64] = inverse[1]
        shared[r][64:72] = jnp.zeros((8, shared[r].shape[1]), jnp.float32)
        shared[r][64:72, 0:128] = piece[0:8]
        shared[r][64:72, 128:256] = piece[8:16]


def in_order(place, shared, rows, matrix):
    for r in range(Y):
        matrix[(place[1] + Y - r) % Y] = shared[r][rows]
    return matrix[...].reshape(Y * 32, -1)


def couple_kernel(place, arrived, *refs):
    shared, (terms, matrix) = refs[:Y], refs[-2:]
    total = jnp.sum(arrived[...], axis=0)
    product = exact_dot(total, in_order(place, shared, slice(0, 32), matrix))
    for z in range(Z):
        terms[z, 0] = product[:, z * 128:(z + 1) * 128]
        terms[z, 1] = total


def latter_kernel(place, arrived, *refs):
    shared, (terms, matrix) = refs[:Y], refs[-2:]
    rhs = sum(piece[64:72] for piece in shared)
    rhs = jnp.concatenate([rhs[:, 0:128], rhs[:, 128:256]], axis=0)
    second = rhs - jnp.sum(arrived[:, 0], axis=0)
    product = exact_dot(second, in_order(place, shared, slice(32, 64), matrix))
    part = lambda z: product[:, (z % Z) * 128:(z % Z + 1) * 128]
    for z in range(Z):
        for k, step in enumerate(NEAR):
            terms[z, k] = part(z + step)


def close_kernel(place, first, arrived, *refs):
    copies = refs[-1]
    latter = jnp.sum(arrived[...], axis=0)
    near = [first[(place[0] + Z + step) % Z, 1] for step in NEAR]
    for target in range(X * C * Y):
        for k in range(QUAD):
            pick = k if k < 3 else 3 + target // Y % C
            copies[target, k] = near[pick]
            copies[target, QUAD + k] = latter[pick]


def around(z):
    return (z % QUAD, (z + 1) % QUAD, (z + 3) % QUAD, (z + 2) % QUAD)


def cut_kernel(place, factor, *refs):
    by_class, by_y, sems = refs[:4], refs[4:8], refs[8]
    classes = around(place[0])
    width = by_y[0].shape[2]
    copies = []
    for r in range(Y):
        for k in range(QUAD):
            strip = pl.multiple_of((classes[k] * Y + (place[1] + r) % Y) * width, width)
            copies.append((factor.at[0, :, pl.ds(strip, width)], by_class[k].at[r]))
            copies.append((factor.at[1, :, pl.ds(strip, width)], by_y[r].at[k]))
    copy_all(copies, sems)


def turn_kernel(*refs):
    arrived, sent, sems = refs[:4], refs[4:8], refs[8]
    copy_all([(arrived[k].at[r], sent[r].at[k]) for r in range(Y) for k in range(QUAD)], sems)


def merge_kernel(place, *refs):
    arrived, sent, sems = refs[:4], refs[4:8], refs[8]
    copy_all([(arrived[r].at[k], sent[k].at[(place[1] + Y - r) % Y]) for r in range(Y) for k in range(QUAD)], sems)


def update_kernel(place, rows, *refs):
    by_r, by_k = refs[:Y], refs[Y:Y + QUAD]
    out, factor, high, low, result, sems = refs[Y + QUAD:]
    start = lambda src, dst, i: pltpu.make_async_copy(src, dst, sems.at[i])
    slots = [(place[1] + Y - r) % Y for r in range(Y)]
    arriving = [start(by_r[r], factor.at[0, r], r) for r in range(Y)]
    arriving += [start(by_k[k], factor.at[1, k], Y + k) for k in range(QUAD)]
    for copy in arriving:
        copy.start()
    left_high, left_low = split(jnp.concatenate([rows[:, k].reshape(-1, 128) for k in range(2 * QUAD)], axis=1))
    for r in range(Y):
        arriving[r].wait()
        high[0, :, slots[r]], low[0, :, slots[r]] = split(factor[0, r])
    for k in range(QUAD):
        arriving[Y + k].wait()
        high[1, k], low[1, k] = split(factor[1, k])
    dot = functools.partial(jnp.dot, preferred_element_type=jnp.float32)
    width = result.shape[2]
    sent = []
    for i, begin in enumerate(range(0, width, 256)):
        at = slice(begin, min(begin + 256, width))
        right_high, right_low = (part[..., at].reshape(2 * QUAD * 128, -1) for part in (high, low))
        product = dot(left_high, right_high) + (dot(left_high, right_low) + dot(left_low, right_high))
        result[..., at] = product.reshape(result.shape[0], 16, -1)
        sent.append(start(result.at[..., at], out.at[..., at], Y + QUAD + i))
        sent[-1].start()
    for copy in sent:
        copy.wait()


def shift_y(value, step):
    return lax.ppermute(value, "y", [(y, (y + step) % Y) for y in range(Y)])


def shift_z(value, step):
    return lax.ppermute(value, "z", [(z, (z + step) % Z) for z in range(Z)])


def shift_far(value):
    pairs = [
        (c * Z + z, c * Z + (z + (2 if c else -2)) % Z) for c in range(C) for z in range(Z)
    ]
    return lax.ppermute(value, ("c", "z"), pairs)


def to_windows(own, up, down, far):
    return own, shift_z(up, 1), shift_z(down, -1), shift_far(far)


def to_ys(own, *others):
    return own, *(shift_y(other, step + 1) for step, other in enumerate(others))


def exchange(value, axes):
    return lax.all_to_all(value, axes, 0, 0, tiled=True)


def body(panel_rhs, diag_inv, coupling, trail_factor, trail_rhs):
    z, y = lax.axis_index("z"), lax.axis_index("y")
    prow = lax.axis_index("x") * C + lax.axis_index("c")
    place = jnp.stack([z, y]).astype(jnp.int32)
    strip, narrow = panel_rhs.shape[0], panel_rhs.shape[2]
    width = trail_rhs.shape[1] // (QUAD * Y)
    block = f32(QUAD, 32, width)
    sems = lambda n: [pltpu.SemaphoreType.DMA((n,))]
    matrix = [pltpu.VMEM((Y, 32, 1024), jnp.float32)]

    rhs = panel_rhs.transpose(1, 0, 2)
    lanes = lax.broadcasted_iota(jnp.int32, (1, 128), 1) // narrow
    second_rhs = jnp.where(lanes == y, jnp.tile(rhs[1], (1, Y)), 0.0)
    terms = call(open_kernel, f32(Z * Y, 16, 128), (rhs[0], diag_inv), VMEM, (VMEM,) * 2)
    arrived = exchange(terms, COLS)
    shared = call(
        share_kernel, (f32(72, 1024),) * Y, (place, second_rhs, diag_inv, coupling),
        (VMEM,) * Y, (SMEM,) + (VMEM,) * 3,
    )
    shared = to_ys(*shared)

    cut = call(
        cut_kernel, (block,) * 8, (place, trail_factor), (ANY,) * 8, (SMEM, VMEM), sems(32), moved=7340032, limit=60,
    )
    by_class, by_y = to_windows(*cut[:4]), to_ys(*cut[4:])

    terms = call(
        couple_kernel, f32(Z, 2, 16, 128), (place, arrived, *shared, cut[0], cut[4]),
        VMEM, (SMEM,) + (VMEM,) * 5 + (ANY,) * 2, matrix, limit=60,
    )
    first = exchange(terms, "z")
    by_r = call(turn_kernel, (block,) * 4, by_class, (ANY,) * 4, (VMEM,) * 4, sems(16), moved=3670016, limit=60)
    first_factor = to_ys(*by_r)

    terms = call(
        latter_kernel, f32(Z, len(NEAR), 16, 128), (place, first, *shared, *by_class[1:], *by_y[1:]),
        VMEM, (SMEM,) + (VMEM,) * 5 + (ANY,) * 6, matrix, limit=60,
    )
    arrived = exchange(terms, "z")
    by_k = call(merge_kernel, (block,) * 4, (place, *by_y), (ANY,) * 4, (SMEM,) + (VMEM,) * 4, sems(16), moved=3670016, limit=60)
    latter_factor = to_windows(*by_k)
    copies = call(close_kernel, f32(X * C * Y, 2 * QUAD, 16, 128), (place, first, arrived, first_factor[1], first_factor[3]), VMEM, (SMEM, VMEM, VMEM, ANY, ANY))
    rows = exchange(copies, SPREAD)

    factor = lambda dtype: pltpu.VMEM((2, QUAD, *block.shape), dtype)
    update = call(
        update_kernel, f32(X * C * Y, 16, width), (place, rows, *first_factor, *latter_factor),
        ANY, (SMEM, VMEM) + (ANY,) * 8,
        [factor(jnp.float32), factor(jnp.bfloat16), factor(jnp.bfloat16), pltpu.VMEM((X * C * Y, 16, width), jnp.float32)] + sems(12),
        flops=2818572288, moved=7602176, limit=56,
    )
    parts = exchange(update, COLS)
    parts = parts.reshape(2, QUAD * Y, *parts.shape[1:])
    reduced = trail_rhs - (parts[0] + parts[1]).transpose(1, 0, 2).reshape(trail_rhs.shape)

    own = lambda panel: lax.dynamic_slice(
        rows, (prow * Y, panel * QUAD, 0, y * narrow), (Y, 1, rows.shape[2], narrow)
    ).reshape(strip, narrow)
    solved = jnp.stack([own(0), own(1)], axis=1)
    return solved, reduced


def solution(mesh):
    devices = Mesh(mesh.devices.reshape(X, C, Z, Y), ("x", "c", "z", "y"))
    placed = (
        P(ROWS, None, COLS),
        P(None, COLS, None),
        P(COLS, None),
        P(None, COLS, ROWS),
        P(COLS, ROWS),
    )
    return jax.shard_map(
        body,
        mesh=devices,
        in_specs=placed,
        out_specs=(P(ROWS, None, COLS), P(COLS, ROWS)),
        check_vma=False,
    )
```

```python
import functools

import jax
import jax.numpy as jnp
from jax import lax
from jax.experimental import pallas as pl
from jax.experimental.pallas import tpu as pltpu
from jax.sharding import Mesh, PartitionSpec as P

X, C, Z, Y = 4, 2, 8, 4
ROWS = ("x", "c")
COLS = ("z", "y")
SPREAD = ("x", "c", "y")
QUAD = 4
NEAR = (0, -1, 1, 2, -2)
SIDES = (0, 1, 3)
VMEM = pl.BlockSpec(memory_space=pltpu.VMEM)
ANY = pl.BlockSpec(memory_space=pl.ANY)
SMEM = pl.BlockSpec(memory_space=pltpu.SMEM)


def f32(*shape):
    return jax.ShapeDtypeStruct(shape, jnp.float32)


def call(kernel, outs, ins, out_specs, in_specs, scratch=(), flops=0, moved=0, limit=16):
    return pl.pallas_call(
        kernel,
        out_shape=outs,
        in_specs=in_specs,
        out_specs=out_specs,
        scratch_shapes=scratch,
        compiler_params=pltpu.CompilerParams(vmem_limit_bytes=limit << 20),
        cost_estimate=pl.CostEstimate(flops=flops, bytes_accessed=moved, transcendentals=0),
    )(*ins)


def exact_dot(left, right):
    return lax.dot_general(
        left, right, (((1,), (0,)), ((), ())),
        precision=lax.Precision.HIGHEST, preferred_element_type=jnp.float32,
    )


def split(value):
    high = value.astype(jnp.bfloat16)
    return high, (value - high.astype(jnp.float32)).astype(jnp.bfloat16)


def copy_all(copies, sems):
    started = [pltpu.make_async_copy(src, dst, sems.at[i]) for i, (src, dst) in enumerate(copies)]
    for copy in started:
        copy.start()
    for copy in started:
        copy.wait()


def open_kernel(rhs, inverse, terms):
    product = exact_dot(rhs[...], inverse[0])
    rows = rhs.shape[0] // Y
    for z in range(Z):
        for y in range(Y):
            terms[z * Y + y] = product[y * rows:(y + 1) * rows, z * 128:(z + 1) * 128]


def share_kernel(place, rhs, inverse, couple, *shared):
    for r in range(Y):
        rows = pl.ds(pl.multiple_of((place[1] + r) % Y * 16, 16), 16)
        piece = rhs[rows]
        shared[r][0:32] = couple[...]
        shared[r][32:64] = inverse[1]
        shared[r][64:72] = jnp.zeros((8, shared[r].shape[1]), jnp.float32)
        shared[r][64:72, 0:128] = piece[0:8]
        shared[r][64:72, 128:256] = piece[8:16]


def in_order(place, shared, rows, matrix):
    for r in range(Y):
        matrix[(place[1] + Y - r) % Y] = shared[r][rows]
    return matrix[...].reshape(Y * 32, -1)


def couple_kernel(place, arrived, *refs):
    shared, (terms, matrix) = refs[:Y], refs[-2:]
    total = jnp.sum(arrived[...], axis=0)
    product = exact_dot(total, in_order(place, shared, slice(0, 32), matrix))
    for z in range(Z):
        terms[z, 0] = product[:, z * 128:(z + 1) * 128]
        terms[z, 1] = total


def latter_kernel(place, arrived, *refs):
    shared, (terms, matrix) = refs[:Y], refs[-2:]
    rhs = sum(piece[64:72] for piece in shared)
    rhs = jnp.concatenate([rhs[:, 0:128], rhs[:, 128:256]], axis=0)
    second = rhs - jnp.sum(arrived[:, 0], axis=0)
    product = exact_dot(second, in_order(place, shared, slice(32, 64), matrix))
    part = lambda z: product[:, (z % Z) * 128:(z % Z + 1) * 128]
    for z in range(Z):
        for k, step in enumerate(NEAR):
            terms[z, k] = part(z + step)


def close_kernel(place, first, arrived, *refs):
    copies = refs[-1]
    latter = jnp.sum(arrived[...], axis=0)
    near = [first[(place[0] + Z + step) % Z, 1] for step in NEAR]
    for target in range(X * C * Y):
        for k in range(QUAD):
            pick = k if k < 3 else 3 + target // Y % C
            copies[target, k] = near[pick]
            copies[target, QUAD + k] = latter[pick]


def around(z):
    return (z % QUAD, (z + 1) % QUAD, (z + 3) % QUAD, (z + 2) % QUAD)


def cut_kernel(place, factor, *refs):
    by_class, by_y, sems = refs[:4], refs[4:8], refs[8]
    classes = around(place[0])
    width = by_y[0].shape[2]
    copies = []
    for r in range(Y):
        for k in range(QUAD):
            strip = pl.multiple_of((classes[k] * Y + (place[1] + r) % Y) * width, width)
            target = by_class[k].at[SIDES.index(r)] if r in SIDES else by_y[r].at[QUAD + k]
            copies.append((factor.at[0, :, pl.ds(strip, width)], target))
            copies.append((factor.at[1, :, pl.ds(strip, width)], by_y[r].at[k]))
    copy_all(copies, sems)


def turn_kernel(*refs):
    arrived, sent, sems = refs[:4], refs[4:7], refs[7]
    copy_all([(arrived[k].at[i], sent[i].at[k]) for i in range(len(SIDES)) for k in range(QUAD)], sems)


def merge_kernel(place, *refs):
    arrived, sent, sems = refs[:4], refs[4:8], refs[8]
    copies = [(arrived[r].at[k], sent[k].at[(place[1] + Y - r) % Y]) for r in range(Y) for k in range(QUAD)]
    copies += [(arrived[2].at[QUAD + k], sent[k].at[Y]) for k in range(QUAD)]
    copy_all(copies, sems)


def update_kernel(place, rows, *refs):
    by_r, by_k = refs[:3], refs[3:3 + QUAD]
    out, sides, classes, high, low, result, sems = refs[3 + QUAD:]
    start = lambda src, dst, i: pltpu.make_async_copy(src, dst, sems.at[i])
    slot = lambda r: (place[1] + Y - r) % Y
    arriving = [start(by_r[i], sides.at[i], i) for i in range(3)]
    arriving += [start(by_k[k], classes.at[k], 3 + k) for k in range(QUAD)]
    for copy in arriving:
        copy.start()
    left_high, left_low = split(jnp.concatenate([rows[:, k].reshape(-1, 128) for k in range(2 * QUAD)], axis=1))
    for i, r in enumerate(SIDES):
        arriving[i].wait()
        high[0, :, slot(r)], low[0, :, slot(r)] = split(sides[i])
    for k in range(QUAD):
        arriving[3 + k].wait()
        high[1, k], low[1, k] = split(classes[k, 0:Y])
        high[0, k, slot(2)], low[0, k, slot(2)] = split(classes[k, Y])
    dot = functools.partial(jnp.dot, preferred_element_type=jnp.float32)
    width = result.shape[2]
    sent = []
    for i, begin in enumerate(range(0, width, 256)):
        at = slice(begin, min(begin + 256, width))
        right_high, right_low = (part[..., at].reshape(2 * QUAD * 128, -1) for part in (high, low))
        product = dot(left_high, right_high) + (dot(left_high, right_low) + dot(left_low, right_high))
        result[..., at] = product.reshape(result.shape[0], 16, -1)
        sent.append(start(result.at[..., at], out.at[..., at], 3 + QUAD + i))
        sent[-1].start()
    for copy in sent:
        copy.wait()


def shift_y(value, step):
    return lax.ppermute(value, "y", [(y, (y + step) % Y) for y in range(Y)])


def shift_z(value, step):
    return lax.ppermute(value, "z", [(z, (z + step) % Z) for z in range(Z)])


def shift_far(value):
    pairs = [
        (c * Z + z, c * Z + (z + (2 if c else -2)) % Z) for c in range(C) for z in range(Z)
    ]
    return lax.ppermute(value, ("c", "z"), pairs)


def to_windows(own, up, down, far):
    return own, shift_z(up, 1), shift_z(down, -1), shift_far(far)


def to_ys(own, *others, steps=(1, 2, 3)):
    return own, *(shift_y(other, step) for step, other in zip(steps, others))


def exchange(value, axes):
    return lax.all_to_all(value, axes, 0, 0, tiled=True)


def body(panel_rhs, diag_inv, coupling, trail_factor, trail_rhs):
    z, y = lax.axis_index("z"), lax.axis_index("y")
    prow = lax.axis_index("x") * C + lax.axis_index("c")
    place = jnp.stack([z, y]).astype(jnp.int32)
    strip, narrow = panel_rhs.shape[0], panel_rhs.shape[2]
    width = trail_rhs.shape[1] // (QUAD * Y)
    block = f32(QUAD, 32, width)
    sems = lambda n: [pltpu.SemaphoreType.DMA((n,))]
    matrix = [pltpu.VMEM((Y, 32, 1024), jnp.float32)]

    rhs = panel_rhs.transpose(1, 0, 2)
    lanes = lax.broadcasted_iota(jnp.int32, (1, 128), 1) // narrow
    second_rhs = jnp.where(lanes == y, jnp.tile(rhs[1], (1, Y)), 0.0)
    terms = call(open_kernel, f32(Z * Y, 16, 128), (rhs[0], diag_inv), VMEM, (VMEM,) * 2)
    arrived = exchange(terms, COLS)
    shared = call(
        share_kernel, (f32(72, 1024),) * Y, (place, second_rhs, diag_inv, coupling),
        (VMEM,) * Y, (SMEM,) + (VMEM,) * 3,
    )
    shared = to_ys(*shared)

    blocks = lambda count: f32(count, 32, width)
    cut = call(
        cut_kernel, (blocks(3),) * 4 + tuple(blocks(8 if r == 2 else 4) for r in range(Y)), (place, trail_factor),
        (ANY,) * 8, (SMEM, VMEM), sems(32), moved=7340032, limit=60,
    )
    by_class, by_y = to_windows(*cut[:4]), to_ys(*cut[4:])

    terms = call(
        couple_kernel, f32(Z, 2, 16, 128), (place, arrived, *shared, cut[0], cut[4]),
        VMEM, (SMEM,) + (VMEM,) * 5 + (ANY,) * 2, matrix, limit=60,
    )
    first = exchange(terms, "z")
    by_r = call(turn_kernel, (block,) * 3, by_class, (ANY,) * 3, (VMEM,) * 4, sems(12), moved=3670016, limit=60)
    first_factor = to_ys(*by_r, steps=SIDES[1:])

    terms = call(
        latter_kernel, f32(Z, len(NEAR), 16, 128), (place, first, *shared, *by_class[1:], *by_y[1:]),
        VMEM, (SMEM,) + (VMEM,) * 5 + (ANY,) * 6, matrix, limit=60,
    )
    arrived = exchange(terms, "z")
    by_k = call(merge_kernel, (blocks(Y + 1),) * 4, (place, *by_y), (ANY,) * 4, (SMEM,) + (VMEM,) * 4, sems(20), moved=3670016, limit=60)
    latter_factor = to_windows(*by_k)
    copies = call(close_kernel, f32(X * C * Y, 2 * QUAD, 16, 128), (place, first, arrived, *first_factor[1:], by_k[0]), VMEM, (SMEM, VMEM, VMEM) + (ANY,) * 3)
    rows = exchange(copies, SPREAD)

    part = pltpu.VMEM((2, QUAD, *block.shape), jnp.bfloat16)
    update = call(
        update_kernel, f32(X * C * Y, 16, width), (place, rows, *first_factor, *latter_factor),
        ANY, (SMEM, VMEM) + (ANY,) * 7,
        [
            pltpu.VMEM((3, *block.shape), jnp.float32),
            pltpu.VMEM((QUAD, Y + 1, 32, width), jnp.float32),
            part,
            part,
            pltpu.VMEM((X * C * Y, 16, width), jnp.float32),
        ] + sems(11),
        flops=2818572288, moved=7602176, limit=56,
    )
    parts = exchange(update, COLS)
    parts = parts.reshape(2, QUAD * Y, *parts.shape[1:])
    reduced = trail_rhs - (parts[0] + parts[1]).transpose(1, 0, 2).reshape(trail_rhs.shape)

    own = lambda panel: lax.dynamic_slice(
        rows, (prow * Y, panel * QUAD, 0, y * narrow), (Y, 1, rows.shape[2], narrow)
    ).reshape(strip, narrow)
    solved = jnp.stack([own(0), own(1)], axis=1)
    return solved, reduced


def solution(mesh):
    devices = Mesh(mesh.devices.reshape(X, C, Z, Y), ("x", "c", "z", "y"))
    placed = (
        P(ROWS, None, COLS),
        P(None, COLS, None),
        P(COLS, None),
        P(None, COLS, ROWS),
        P(COLS, ROWS),
    )
    return jax.shard_map(
        body,
        mesh=devices,
        in_specs=placed,
        out_specs=(P(ROWS, None, COLS), P(COLS, ROWS)),
        check_vma=False,
    )
```

```python
import functools

import jax
import jax.numpy as jnp
from jax import lax
from jax.experimental import pallas as pl
from jax.experimental.pallas import tpu as pltpu
from jax.sharding import Mesh, PartitionSpec as P

X, C, Z, Y = 4, 2, 8, 4
ROWS = ("x", "c")
COLS = ("z", "y")
SPREAD = ("x", "c", "y")
QUAD = 4
NEAR = (0, -1, 1, 2, -2)
VMEM = pl.BlockSpec(memory_space=pltpu.VMEM)
ANY = pl.BlockSpec(memory_space=pl.ANY)
SMEM = pl.BlockSpec(memory_space=pltpu.SMEM)


def f32(*shape):
    return jax.ShapeDtypeStruct(shape, jnp.float32)


def call(kernel, outs, ins, out_specs, in_specs, scratch=(), flops=0, moved=0, limit=16):
    return pl.pallas_call(
        kernel,
        out_shape=outs,
        in_specs=in_specs,
        out_specs=out_specs,
        scratch_shapes=scratch,
        compiler_params=pltpu.CompilerParams(vmem_limit_bytes=limit << 20),
        cost_estimate=pl.CostEstimate(flops=flops, bytes_accessed=moved, transcendentals=0),
    )(*ins)


def exact_dot(left, right):
    return lax.dot_general(
        left, right, (((1,), (0,)), ((), ())),
        precision=lax.Precision.HIGHEST, preferred_element_type=jnp.float32,
    )


def split(value):
    high = value.astype(jnp.bfloat16)
    return high, (value - high.astype(jnp.float32)).astype(jnp.bfloat16)


def copy_all(copies, sems):
    started = [pltpu.make_async_copy(src, dst, sems.at[i]) for i, (src, dst) in enumerate(copies)]
    for copy in started:
        copy.start()
    for copy in started:
        copy.wait()


def open_kernel(rhs, inverse, terms):
    product = exact_dot(rhs[...], inverse[0])
    rows = rhs.shape[0] // Y
    for z in range(Z):
        for y in range(Y):
            terms[z * Y + y] = product[y * rows:(y + 1) * rows, z * 128:(z + 1) * 128]


def share_kernel(place, rhs, inverse, couple, *shared):
    for r in range(Y):
        rows = pl.ds(pl.multiple_of((place[1] + r) % Y * 16, 16), 16)
        piece = rhs[rows]
        shared[r][0:32] = couple[...]
        shared[r][32:64] = inverse[1]
        shared[r][64:72] = jnp.zeros((8, shared[r].shape[1]), jnp.float32)
        shared[r][64:72, 0:128] = piece[0:8]
        shared[r][64:72, 128:256] = piece[8:16]


def in_order(place, shared, rows, matrix):
    for r in range(Y):
        matrix[(place[1] + Y - r) % Y] = shared[r][rows]
    return matrix[...].reshape(Y * 32, -1)


def couple_kernel(place, arrived, *refs):
    shared, (terms, matrix) = refs[:Y], refs[-2:]
    total = jnp.sum(arrived[...], axis=0)
    product = exact_dot(total, in_order(place, shared, slice(0, 32), matrix))
    for z in range(Z):
        terms[z, 0] = product[:, z * 128:(z + 1) * 128]
        terms[z, 1] = total


def latter_kernel(place, arrived, *refs):
    shared, (terms, matrix) = refs[:Y], refs[-2:]
    rhs = sum(piece[64:72] for piece in shared)
    rhs = jnp.concatenate([rhs[:, 0:128], rhs[:, 128:256]], axis=0)
    second = rhs - jnp.sum(arrived[:, 0], axis=0)
    product = exact_dot(second, in_order(place, shared, slice(32, 64), matrix))
    part = lambda z: product[:, (z % Z) * 128:(z % Z + 1) * 128]
    for z in range(Z):
        for k, step in enumerate(NEAR):
            terms[z, k] = part(z + step)


def close_kernel(place, first, arrived, *refs):
    copies = refs[-1]
    latter = jnp.sum(arrived[...], axis=0)
    near = [first[(place[0] + Z + step) % Z, 1] for step in NEAR]
    for target in range(X * C * Y):
        for k in range(QUAD):
            pick = k if k < 3 else 3 + target // Y % C
            copies[target, k] = near[pick]
            copies[target, QUAD + k] = latter[pick]


def around(z):
    return (z % QUAD, (z + 1) % QUAD, (z + 3) % QUAD, (z + 2) % QUAD)


def cut_kernel(place, factor, *refs):
    by_class, by_y, sems = refs[:4], refs[4:8], refs[8]
    classes = around(place[0])
    width = by_y[0].shape[2]
    copies = []
    for r in range(Y):
        for k in range(QUAD):
            strip = pl.multiple_of((classes[k] * Y + (place[1] + r) % Y) * width, width)
            copies.append((factor.at[0, :, pl.ds(strip, width)], by_class[k].at[r]))
            copies.append((factor.at[1, :, pl.ds(strip, width)], by_y[r].at[k]))
    copy_all(copies, sems)


def turn_kernel(*refs):
    arrived, sent, sems = refs[:4], refs[4:8], refs[8]
    copy_all([(arrived[k].at[r], sent[r].at[k]) for r in range(Y) for k in range(QUAD)], sems)


def merge_kernel(place, *refs):
    arrived, sent, sems = refs[:4], refs[4:8], refs[8]
    copy_all([(arrived[r].at[k], sent[k].at[(place[1] + Y - r) % Y]) for r in range(Y) for k in range(QUAD)], sems)


def update_kernel(place, rows, *refs):
    by_r, by_k = refs[:Y], refs[Y:Y + QUAD]
    out, factor, high, low, result, sems = refs[Y + QUAD:]
    start = lambda src, dst, i: pltpu.make_async_copy(src, dst, sems.at[i])
    slots = [(place[1] + Y - r) % Y for r in range(Y)]
    arriving = [start(by_r[r], factor.at[0, r], r) for r in range(Y)]
    arriving += [start(by_k[k], factor.at[1, k], Y + k) for k in range(QUAD)]
    for copy in arriving:
        copy.start()
    left_high, left_low = split(jnp.concatenate([rows[:, k].reshape(-1, 128) for k in range(2 * QUAD)], axis=1))
    for r in range(Y):
        arriving[r].wait()
        high[0, :, slots[r]], low[0, :, slots[r]] = split(factor[0, r])
    for k in range(QUAD):
        arriving[Y + k].wait()
        high[1, k], low[1, k] = split(factor[1, k])
    dot = functools.partial(jnp.dot, preferred_element_type=jnp.float32)
    width = result.shape[2]
    sent = []
    for i, begin in enumerate(range(0, width, 256)):
        at = slice(begin, min(begin + 256, width))
        right_high, right_low = (part[..., at].reshape(2 * QUAD * 128, -1) for part in (high, low))
        product = dot(left_high, right_high) + (dot(left_high, right_low) + dot(left_low, right_high))
        result[..., at] = product.reshape(result.shape[0], 16, -1)
        sent.append(start(result.at[..., at], out.at[..., at], Y + QUAD + i))
        sent[-1].start()
    for copy in sent:
        copy.wait()


def shift_y(value, step):
    return lax.ppermute(value, "y", [(y, (y + step) % Y) for y in range(Y)])


def shift_z(value, step):
    return lax.ppermute(value, "z", [(z, (z + step) % Z) for z in range(Z)])


def shift_far(value):
    pairs = [
        (c * Z + z, c * Z + (z + (2 if c else -2)) % Z) for c in range(C) for z in range(Z)
    ]
    return lax.ppermute(value, ("c", "z"), pairs)


def to_windows(own, up, down, far):
    return own, shift_z(up, 1), shift_z(down, -1), shift_far(far)


def to_ys(own, *others):
    return own, *(shift_y(other, step + 1) for step, other in enumerate(others))


def exchange(value, axes):
    return lax.all_to_all(value, axes, 0, 0, tiled=True)


def body(panel_rhs, diag_inv, coupling, trail_factor, trail_rhs):
    z, y = lax.axis_index("z"), lax.axis_index("y")
    prow = lax.axis_index("x") * C + lax.axis_index("c")
    place = jnp.stack([z, y]).astype(jnp.int32)
    strip, narrow = panel_rhs.shape[0], panel_rhs.shape[2]
    width = trail_rhs.shape[1] // (QUAD * Y)
    block = f32(QUAD, 32, width)
    sems = lambda n: [pltpu.SemaphoreType.DMA((n,))]
    matrix = [pltpu.VMEM((Y, 32, 1024), jnp.float32)]

    rhs = panel_rhs.transpose(1, 0, 2)
    lanes = lax.broadcasted_iota(jnp.int32, (1, 128), 1) // narrow
    second_rhs = jnp.where(lanes == y, jnp.tile(rhs[1], (1, Y)), 0.0)
    terms = call(open_kernel, f32(Z * Y, 16, 128), (rhs[0], diag_inv), VMEM, (VMEM,) * 2)
    arrived = exchange(terms, COLS)
    shared = call(
        share_kernel, (f32(72, 1024),) * Y, (place, second_rhs, diag_inv, coupling),
        (VMEM,) * Y, (SMEM,) + (VMEM,) * 3,
    )
    shared = to_ys(*shared)

    cut = call(
        cut_kernel, (block,) * 8, (place, trail_factor), (ANY,) * 8, (SMEM, VMEM), sems(32), moved=7340032, limit=60,
    )
    by_class, by_y = to_windows(*cut[:4]), to_ys(*cut[4:])

    terms = call(
        couple_kernel, f32(Z, 2, 16, 128), (place, arrived, *shared, cut[0], cut[4]),
        VMEM, (SMEM,) + (VMEM,) * 5 + (ANY,) * 2, matrix, limit=60,
    )
    first = exchange(terms, "z")
    by_r = call(turn_kernel, (block,) * 4, by_class, (ANY,) * 4, (VMEM,) * 4, sems(16), moved=3670016, limit=60)
    first_factor = to_ys(*by_r)

    terms = call(
        latter_kernel, f32(Z, len(NEAR), 16, 128), (place, first, *shared, *by_class[1:], *by_y[1:]),
        VMEM, (SMEM,) + (VMEM,) * 5 + (ANY,) * 6, matrix, limit=60,
    )
    arrived = exchange(terms, "z")
    by_k = call(merge_kernel, (block,) * 4, (place, *by_y), (ANY,) * 4, (SMEM,) + (VMEM,) * 4, sems(16), moved=3670016, limit=60)
    latter_factor = to_windows(*by_k)
    copies = call(close_kernel, f32(X * C * Y, 2 * QUAD, 16, 128), (place, first, arrived, first_factor[2], first_factor[3], by_k[0]), VMEM, (SMEM, VMEM, VMEM) + (ANY,) * 3)
    rows = exchange(copies, SPREAD)

    factor = lambda dtype: pltpu.VMEM((2, QUAD, *block.shape), dtype)
    update = call(
        update_kernel, f32(X * C * Y, 16, width), (place, rows, *first_factor, *latter_factor),
        ANY, (SMEM, VMEM) + (ANY,) * 8,
        [factor(jnp.float32), factor(jnp.bfloat16), factor(jnp.bfloat16), pltpu.VMEM((X * C * Y, 16, width), jnp.float32)] + sems(12),
        flops=2818572288, moved=7602176, limit=56,
    )
    parts = exchange(update, COLS)
    parts = parts.reshape(2, QUAD * Y, *parts.shape[1:])
    reduced = trail_rhs - (parts[0] + parts[1]).transpose(1, 0, 2).reshape(trail_rhs.shape)

    own = lambda panel: lax.dynamic_slice(
        rows, (prow * Y, panel * QUAD, 0, y * narrow), (Y, 1, rows.shape[2], narrow)
    ).reshape(strip, narrow)
    solved = jnp.stack([own(0), own(1)], axis=1)
    return solved, reduced


def solution(mesh):
    devices = Mesh(mesh.devices.reshape(X, C, Z, Y), ("x", "c", "z", "y"))
    placed = (
        P(ROWS, None, COLS),
        P(None, COLS, None),
        P(COLS, None),
        P(None, COLS, ROWS),
        P(COLS, ROWS),
    )
    return jax.shard_map(
        body,
        mesh=devices,
        in_specs=placed,
        out_specs=(P(ROWS, None, COLS), P(COLS, ROWS)),
        check_vma=False,
    )
```

```python
import functools

import jax
import jax.numpy as jnp
from jax import lax
from jax.experimental import pallas as pl
from jax.experimental.pallas import tpu as pltpu
from jax.sharding import Mesh, PartitionSpec as P

X, C, Z, Y = 4, 2, 8, 4
ROWS = ("x", "c")
COLS = ("z", "y")
SPREAD = ("x", "c", "y")
QUAD = 4
NEAR = (0, -1, 1, 2, -2)
SIDES = ((0, 0), (0, 1), (0, 3), (1, 0))
OTHERS = ((1, 1), (1, 2), (1, 3), (0, 2))
VMEM = pl.BlockSpec(memory_space=pltpu.VMEM)
ANY = pl.BlockSpec(memory_space=pl.ANY)
SMEM = pl.BlockSpec(memory_space=pltpu.SMEM)


def f32(*shape):
    return jax.ShapeDtypeStruct(shape, jnp.float32)


def call(kernel, outs, ins, out_specs, in_specs, scratch=(), flops=0, moved=0, limit=16):
    return pl.pallas_call(
        kernel,
        out_shape=outs,
        in_specs=in_specs,
        out_specs=out_specs,
        scratch_shapes=scratch,
        compiler_params=pltpu.CompilerParams(vmem_limit_bytes=limit << 20),
        cost_estimate=pl.CostEstimate(flops=flops, bytes_accessed=moved, transcendentals=0),
    )(*ins)


def exact_dot(left, right):
    return lax.dot_general(
        left, right, (((1,), (0,)), ((), ())),
        precision=lax.Precision.HIGHEST, preferred_element_type=jnp.float32,
    )


def split(value):
    high = value.astype(jnp.bfloat16)
    return high, (value - high.astype(jnp.float32)).astype(jnp.bfloat16)


def copy_all(copies, sems):
    started = [pltpu.make_async_copy(src, dst, sems.at[i]) for i, (src, dst) in enumerate(copies)]
    for copy in started:
        copy.start()
    for copy in started:
        copy.wait()


def open_kernel(rhs, inverse, terms):
    product = exact_dot(rhs[...], inverse[0])
    rows = rhs.shape[0] // Y
    for z in range(Z):
        for y in range(Y):
            terms[z * Y + y] = product[y * rows:(y + 1) * rows, z * 128:(z + 1) * 128]


def share_kernel(place, rhs, inverse, couple, *shared):
    for r in range(Y):
        rows = pl.ds(pl.multiple_of((place[1] + r) % Y * 16, 16), 16)
        piece = rhs[rows]
        shared[r][0:32] = couple[...]
        shared[r][32:64] = inverse[1]
        shared[r][64:72] = jnp.zeros((8, shared[r].shape[1]), jnp.float32)
        shared[r][64:72, 0:128] = piece[0:8]
        shared[r][64:72, 128:256] = piece[8:16]


def in_order(place, shared, rows, matrix):
    for r in range(Y):
        matrix[(place[1] + Y - r) % Y] = shared[r][rows]
    return matrix[...].reshape(Y * 32, -1)


def couple_kernel(place, arrived, *refs):
    shared, (terms, matrix) = refs[:Y], refs[-2:]
    total = jnp.sum(arrived[...], axis=0)
    product = exact_dot(total, in_order(place, shared, slice(0, 32), matrix))
    for z in range(Z):
        terms[z, 0] = product[:, z * 128:(z + 1) * 128]
        terms[z, 1] = total


def latter_kernel(place, arrived, *refs):
    shared, (terms, matrix) = refs[:Y], refs[-2:]
    rhs = sum(piece[64:72] for piece in shared)
    rhs = jnp.concatenate([rhs[:, 0:128], rhs[:, 128:256]], axis=0)
    second = rhs - jnp.sum(arrived[:, 0], axis=0)
    product = exact_dot(second, in_order(place, shared, slice(32, 64), matrix))
    part = lambda z: product[:, (z % Z) * 128:(z % Z + 1) * 128]
    for z in range(Z):
        for k, step in enumerate(NEAR):
            terms[z, k] = part(z + step)


def close_kernel(place, first, arrived, *refs):
    copies = refs[-1]
    latter = jnp.sum(arrived[...], axis=0)
    near = [first[(place[0] + Z + step) % Z, 1] for step in NEAR]
    for target in range(X * C * Y):
        for k in range(QUAD):
            pick = k if k < 3 else 3 + target // Y % C
            copies[target, k] = near[pick]
            copies[target, QUAD + k] = latter[pick]


def around(z):
    return (z % QUAD, (z + 1) % QUAD, (z + 3) % QUAD, (z + 2) % QUAD)


def cut_kernel(place, factor, *refs):
    by_class, by_y, sems = refs[:4], refs[4:8], refs[8]
    classes = around(place[0])
    width = by_y[0].shape[2]
    copies = []
    for k in range(QUAD):
        targets = [by_class[k].at[i] for i in range(4)] + [by_y[i].at[k] for i in range(4)]
        for (panel, r), target in zip(SIDES + OTHERS, targets):
            strip = pl.multiple_of((classes[k] * Y + (place[1] + r) % Y) * width, width)
            copies.append((factor.at[panel, :, pl.ds(strip, width)], target))
    copy_all(copies, sems)


def turn_kernel(*refs):
    arrived, sent, sems = refs[:4], refs[4:8], refs[8]
    copy_all([(arrived[a].at[b], sent[b].at[a]) for b in range(4) for a in range(4)], sems)


def update_kernel(place, rows, *refs):
    blocks = refs[:8]
    out, factor, high, low, result, sems = refs[8:]
    start = lambda src, dst, i: pltpu.make_async_copy(src, dst, sems.at[i])
    slot = lambda r: (place[1] + Y - r) % Y
    arriving = [start(blocks[i], factor.at[i], i) for i in range(8)]
    for copy in arriving:
        copy.start()
    left_high, left_low = split(jnp.concatenate([rows[:, k].reshape(-1, 128) for k in range(2 * QUAD)], axis=1))
    for i, (panel, r) in enumerate(SIDES):
        arriving[i].wait()
        high[panel, :, slot(r)], low[panel, :, slot(r)] = split(factor[i])
    for k in range(QUAD):
        arriving[4 + k].wait()
        for i, (panel, r) in enumerate(OTHERS):
            high[panel, k, slot(r)], low[panel, k, slot(r)] = split(factor[4 + k, i])
    dot = functools.partial(jnp.dot, preferred_element_type=jnp.float32)
    width = result.shape[2]
    sent = []
    for i, begin in enumerate(range(0, width, 256)):
        at = slice(begin, min(begin + 256, width))
        right_high, right_low = (part[..., at].reshape(2 * QUAD * 128, -1) for part in (high, low))
        product = dot(left_high, right_high) + (dot(left_high, right_low) + dot(left_low, right_high))
        result[..., at] = product.reshape(result.shape[0], 16, -1)
        sent.append(start(result.at[..., at], out.at[..., at], 8 + i))
        sent[-1].start()
    for copy in sent:
        copy.wait()


def shift_y(value, step):
    return lax.ppermute(value, "y", [(y, (y + step) % Y) for y in range(Y)])


def shift_z(value, step):
    return lax.ppermute(value, "z", [(z, (z + step) % Z) for z in range(Z)])


def shift_far(value):
    pairs = [
        (c * Z + z, c * Z + (z + (2 if c else -2)) % Z) for c in range(C) for z in range(Z)
    ]
    return lax.ppermute(value, ("c", "z"), pairs)


def to_windows(own, up, down, far):
    return own, shift_z(up, 1), shift_z(down, -1), shift_far(far)


def exchange(value, axes):
    return lax.all_to_all(value, axes, 0, 0, tiled=True)


def body(panel_rhs, diag_inv, coupling, trail_factor, trail_rhs):
    z, y = lax.axis_index("z"), lax.axis_index("y")
    prow = lax.axis_index("x") * C + lax.axis_index("c")
    place = jnp.stack([z, y]).astype(jnp.int32)
    strip, narrow = panel_rhs.shape[0], panel_rhs.shape[2]
    width = trail_rhs.shape[1] // (QUAD * Y)
    block = f32(QUAD, 32, width)
    sems = lambda n: [pltpu.SemaphoreType.DMA((n,))]
    matrix = [pltpu.VMEM((Y, 32, 1024), jnp.float32)]

    rhs = panel_rhs.transpose(1, 0, 2)
    lanes = lax.broadcasted_iota(jnp.int32, (1, 128), 1) // narrow
    second_rhs = jnp.where(lanes == y, jnp.tile(rhs[1], (1, Y)), 0.0)
    terms = call(open_kernel, f32(Z * Y, 16, 128), (rhs[0], diag_inv), VMEM, (VMEM,) * 2)
    arrived = exchange(terms, COLS)
    shared = call(
        share_kernel, (f32(72, 1024),) * Y, (place, second_rhs, diag_inv, coupling),
        (VMEM,) * Y, (SMEM,) + (VMEM,) * 3,
    )
    shared = [shared[0]] + [shift_y(shared[r], r) for r in range(1, Y)]

    cut = call(
        cut_kernel, (block,) * 8, (place, trail_factor), (ANY,) * 8, (SMEM, VMEM), sems(32), moved=7340032, limit=60,
    )
    by_class = to_windows(*cut[:4])
    by_y = [shift_y(piece, r) for piece, (_, r) in zip(cut[4:], OTHERS)]

    terms = call(
        couple_kernel, f32(Z, 2, 16, 128), (place, arrived, *shared, cut[0], cut[4]),
        VMEM, (SMEM,) + (VMEM,) * 5 + (ANY,) * 2, matrix, limit=60,
    )
    first = exchange(terms, "z")
    by_r = call(turn_kernel, (block,) * 4, by_class, (ANY,) * 4, (VMEM,) * 4, sems(16), moved=3670016, limit=60)
    first_factor = [shift_y(piece, r) if r else piece for piece, (_, r) in zip(by_r, SIDES)]

    terms = call(
        latter_kernel, f32(Z, len(NEAR), 16, 128), (place, first, *shared, *by_class[1:], *by_y),
        VMEM, (SMEM,) + (VMEM,) * 5 + (ANY,) * 7, matrix, limit=60,
    )
    arrived = exchange(terms, "z")
    by_k = call(turn_kernel, (block,) * 4, by_y, (ANY,) * 4, (VMEM,) * 4, sems(16), moved=3670016, limit=60)
    latter_factor = to_windows(*by_k)
    copies = call(close_kernel, f32(X * C * Y, 2 * QUAD, 16, 128), (place, first, arrived, first_factor[1], first_factor[2]), VMEM, (SMEM, VMEM, VMEM, ANY, ANY))
    rows = exchange(copies, SPREAD)

    part = pltpu.VMEM((2, QUAD, *block.shape), jnp.bfloat16)
    update = call(
        update_kernel, f32(X * C * Y, 16, width), (place, rows, *first_factor, *latter_factor),
        ANY, (SMEM, VMEM) + (ANY,) * 8,
        [pltpu.VMEM((8, *block.shape), jnp.float32), part, part, pltpu.VMEM((X * C * Y, 16, width), jnp.float32)] + sems(12),
        flops=2818572288, moved=7602176, limit=56,
    )
    parts = exchange(update, COLS)
    parts = parts.reshape(2, QUAD * Y, *parts.shape[1:])
    reduced = trail_rhs - (parts[0] + parts[1]).transpose(1, 0, 2).reshape(trail_rhs.shape)

    own = lambda panel: lax.dynamic_slice(
        rows, (prow * Y, panel * QUAD, 0, y * narrow), (Y, 1, rows.shape[2], narrow)
    ).reshape(strip, narrow)
    solved = jnp.stack([own(0), own(1)], axis=1)
    return solved, reduced


def solution(mesh):
    devices = Mesh(mesh.devices.reshape(X, C, Z, Y), ("x", "c", "z", "y"))
    placed = (
        P(ROWS, None, COLS),
        P(None, COLS, None),
        P(COLS, None),
        P(None, COLS, ROWS),
        P(COLS, ROWS),
    )
    return jax.shard_map(
        body,
        mesh=devices,
        in_specs=placed,
        out_specs=(P(ROWS, None, COLS), P(COLS, ROWS)),
        check_vma=False,
    )
```

```python
import functools

import jax
import jax.numpy as jnp
from jax import lax
from jax.experimental import pallas as pl
from jax.experimental.pallas import tpu as pltpu
from jax.sharding import Mesh, PartitionSpec as P

X, C, Z, Y = 4, 2, 8, 4
ROWS = ("x", "c")
COLS = ("z", "y")
SPREAD = ("x", "c", "y")
QUAD = 4
NEAR = (0, -1, 1, 2, -2)
SIDES = ((0, 0), (0, 1), (0, 3), (1, 0))
OTHERS = ((1, 1), (1, 2), (1, 3), (0, 2))
VMEM = pl.BlockSpec(memory_space=pltpu.VMEM)
ANY = pl.BlockSpec(memory_space=pl.ANY)
SMEM = pl.BlockSpec(memory_space=pltpu.SMEM)


def f32(*shape):
    return jax.ShapeDtypeStruct(shape, jnp.float32)


def call(kernel, outs, ins, out_specs, in_specs, scratch=(), flops=0, moved=0, limit=16):
    return pl.pallas_call(
        kernel,
        out_shape=outs,
        in_specs=in_specs,
        out_specs=out_specs,
        scratch_shapes=scratch,
        compiler_params=pltpu.CompilerParams(vmem_limit_bytes=limit << 20),
        cost_estimate=pl.CostEstimate(flops=flops, bytes_accessed=moved, transcendentals=0),
    )(*ins)


def exact_dot(left, right):
    return lax.dot_general(
        left, right, (((1,), (0,)), ((), ())),
        precision=lax.Precision.HIGHEST, preferred_element_type=jnp.float32,
    )


def split(value):
    high = value.astype(jnp.bfloat16)
    return high, (value - high.astype(jnp.float32)).astype(jnp.bfloat16)


def copy_all(copies, sems):
    started = [pltpu.make_async_copy(src, dst, sems.at[i]) for i, (src, dst) in enumerate(copies)]
    for copy in started:
        copy.start()
    for copy in started:
        copy.wait()


def open_kernel(rhs, inverse, terms):
    product = exact_dot(rhs[...], inverse[0])
    rows = rhs.shape[0] // Y
    for z in range(Z):
        for y in range(Y):
            terms[z * Y + y] = product[y * rows:(y + 1) * rows, z * 128:(z + 1) * 128]


def share_kernel(place, rhs, inverse, couple, *shared):
    for r in range(Y):
        rows = pl.ds(pl.multiple_of((place[1] + r) % Y * 16, 16), 16)
        piece = rhs[rows]
        shared[r][0:32] = couple[...]
        shared[r][32:64] = inverse[1]
        shared[r][64:72] = jnp.zeros((8, shared[r].shape[1]), jnp.float32)
        shared[r][64:72, 0:128] = piece[0:8]
        shared[r][64:72, 128:256] = piece[8:16]


def in_order(place, shared, rows, matrix):
    for r in range(Y):
        matrix[(place[1] + Y - r) % Y] = shared[r][rows]
    return matrix[...].reshape(Y * 32, -1)


def couple_kernel(place, arrived, *refs):
    shared, (terms, matrix) = refs[:Y], refs[-2:]
    total = jnp.sum(arrived[...], axis=0)
    product = exact_dot(total, in_order(place, shared, slice(0, 32), matrix))
    for z in range(Z):
        terms[z, 0] = product[:, z * 128:(z + 1) * 128]
        terms[z, 1] = total


def latter_kernel(place, arrived, *refs):
    shared, (terms, matrix) = refs[:Y], refs[-2:]
    rhs = sum(piece[64:72] for piece in shared)
    rhs = jnp.concatenate([rhs[:, 0:128], rhs[:, 128:256]], axis=0)
    second = rhs - jnp.sum(arrived[:, 0], axis=0)
    product = exact_dot(second, in_order(place, shared, slice(32, 64), matrix))
    part = lambda z: product[:, (z % Z) * 128:(z % Z + 1) * 128]
    for z in range(Z):
        for k, step in enumerate(NEAR):
            terms[z, k] = part(z + step)


def close_kernel(place, first, arrived, *refs):
    copies = refs[-1]
    latter = jnp.sum(arrived[...], axis=0)
    near = [first[(place[0] + Z + step) % Z, 1] for step in NEAR]
    for target in range(X * C * Y):
        for k in range(QUAD):
            pick = k if k < 3 else 3 + target // Y % C
            copies[target, k] = near[pick]
            copies[target, QUAD + k] = latter[pick]


def around(z):
    return (z % QUAD, (z + 1) % QUAD, (z + 3) % QUAD, (z + 2) % QUAD)


def cut_kernel(place, factor, *refs):
    by_class, by_y, sems = refs[:4], refs[4:8], refs[8]
    classes = around(place[0])
    width = by_y[0].shape[2]
    copies = []
    for k in range(QUAD):
        targets = [by_class[k].at[i] for i in range(4)] + [by_y[i].at[k] for i in range(4)]
        for (panel, r), target in zip(SIDES + OTHERS, targets):
            strip = pl.multiple_of((classes[k] * Y + (place[1] + r) % Y) * width, width)
            copies.append((factor.at[panel, :, pl.ds(strip, width)], target))
    copy_all(copies, sems)


def turn_kernel(*refs):
    arrived, sent, sems = refs[:4], refs[4:8], refs[8]
    copy_all([(arrived[a].at[b], sent[b].at[a]) for b in range(4) for a in range(4)], sems)


def update_kernel(place, rows, *refs):
    blocks = refs[:8]
    out, factor, high, low, result, sems = refs[8:]
    start = lambda src, dst, i: pltpu.make_async_copy(src, dst, sems.at[i])
    slot = lambda r: (place[1] + Y - r) % Y
    arriving = [start(blocks[i], factor.at[i], i) for i in range(8)]
    for copy in arriving:
        copy.start()
    left_high, left_low = split(jnp.concatenate([rows[:, k].reshape(-1, 128) for k in range(2 * QUAD)], axis=1))
    for i, (panel, r) in enumerate(SIDES):
        arriving[i].wait()
        high[panel, :, slot(r)], low[panel, :, slot(r)] = split(factor[i])
    for k in range(QUAD):
        arriving[4 + k].wait()
        for i, (panel, r) in enumerate(OTHERS):
            high[panel, k, slot(r)], low[panel, k, slot(r)] = split(factor[4 + k, i])
    dot = functools.partial(jnp.dot, preferred_element_type=jnp.float32)
    width = result.shape[2]
    sent = []
    for i, begin in enumerate(range(0, width, 256)):
        at = slice(begin, min(begin + 256, width))
        right_high, right_low = (part[..., at].reshape(2 * QUAD * 128, -1) for part in (high, low))
        product = dot(left_high, right_high) + (dot(left_high, right_low) + dot(left_low, right_high))
        result[..., at] = product.reshape(result.shape[0], 16, -1)
        sent.append(start(result.at[..., at], out.at[..., at], 8 + i))
        sent[-1].start()
    for copy in sent:
        copy.wait()


def shift_y(value, step):
    return lax.ppermute(value, "y", [(y, (y + step) % Y) for y in range(Y)])


def shift_z(value, step):
    return lax.ppermute(value, "z", [(z, (z + step) % Z) for z in range(Z)])


def shift_far(value):
    pairs = [
        (c * Z + z, c * Z + (z + (2 if c else -2)) % Z) for c in range(C) for z in range(Z)
    ]
    return lax.ppermute(value, ("c", "z"), pairs)


def to_windows(own, up, down, far):
    return own, shift_z(up, 1), shift_z(down, -1), shift_far(far)


def exchange(value, axes):
    return lax.all_to_all(value, axes, 0, 0, tiled=True)


def body(panel_rhs, diag_inv, coupling, trail_factor, trail_rhs):
    z, y = lax.axis_index("z"), lax.axis_index("y")
    prow = lax.axis_index("x") * C + lax.axis_index("c")
    place = jnp.stack([z, y]).astype(jnp.int32)
    strip, narrow = panel_rhs.shape[0], panel_rhs.shape[2]
    width = trail_rhs.shape[1] // (QUAD * Y)
    block = f32(QUAD, 32, width)
    sems = lambda n: [pltpu.SemaphoreType.DMA((n,))]
    matrix = [pltpu.VMEM((Y, 32, 1024), jnp.float32)]

    rhs = panel_rhs.transpose(1, 0, 2)
    lanes = lax.broadcasted_iota(jnp.int32, (1, 128), 1) // narrow
    second_rhs = jnp.where(lanes == y, jnp.tile(rhs[1], (1, Y)), 0.0)
    terms = call(open_kernel, f32(Z * Y, 16, 128), (rhs[0], diag_inv), VMEM, (VMEM,) * 2)
    arrived = exchange(terms, COLS)
    shared = call(
        share_kernel, (f32(72, 1024),) * Y, (place, second_rhs, diag_inv, coupling),
        (VMEM,) * Y, (SMEM,) + (VMEM,) * 3,
    )
    shared = [shared[0]] + [shift_y(shared[r], r) for r in range(1, Y)]

    cut = call(
        cut_kernel, (block,) * 8, (place, trail_factor), (ANY,) * 8, (SMEM, VMEM), sems(32), moved=7340032, limit=60,
    )
    by_class = to_windows(*cut[:4])
    by_y = [shift_y(piece, r) for piece, (_, r) in zip(cut[4:], OTHERS)]

    terms = call(
        couple_kernel, f32(Z, 2, 16, 128), (place, arrived, *shared, cut[0], cut[4]),
        VMEM, (SMEM,) + (VMEM,) * 5 + (ANY,) * 2, matrix, limit=60,
    )
    first = exchange(terms, "z")
    by_r = call(turn_kernel, (block,) * 4, by_class, (ANY,) * 4, (VMEM,) * 4, sems(16), moved=3670016, limit=60)
    first_factor = [shift_y(piece, r) if r else piece for piece, (_, r) in zip(by_r, SIDES)]

    terms = call(
        latter_kernel, f32(Z, len(NEAR), 16, 128), (place, first, *shared, *by_class[1:], *by_y[1:]),
        VMEM, (SMEM,) + (VMEM,) * 5 + (ANY,) * 6, matrix, limit=60,
    )
    arrived = exchange(terms, "z")
    by_k = call(turn_kernel, (block,) * 4, by_y, (ANY,) * 4, (VMEM,) * 4, sems(16), moved=3670016, limit=60)
    latter_factor = to_windows(*by_k)
    copies = call(close_kernel, f32(X * C * Y, 2 * QUAD, 16, 128), (place, first, arrived, first_factor[1], first_factor[2]), VMEM, (SMEM, VMEM, VMEM, ANY, ANY))
    rows = exchange(copies, SPREAD)

    part = pltpu.VMEM((2, QUAD, *block.shape), jnp.bfloat16)
    update = call(
        update_kernel, f32(X * C * Y, 16, width), (place, rows, *first_factor, *latter_factor),
        ANY, (SMEM, VMEM) + (ANY,) * 8,
        [pltpu.VMEM((8, *block.shape), jnp.float32), part, part, pltpu.VMEM((X * C * Y, 16, width), jnp.float32)] + sems(12),
        flops=2818572288, moved=7602176, limit=56,
    )
    parts = exchange(update, COLS)
    parts = parts.reshape(2, QUAD * Y, *parts.shape[1:])
    reduced = trail_rhs - (parts[0] + parts[1]).transpose(1, 0, 2).reshape(trail_rhs.shape)

    own = lambda panel: lax.dynamic_slice(
        rows, (prow * Y, panel * QUAD, 0, y * narrow), (Y, 1, rows.shape[2], narrow)
    ).reshape(strip, narrow)
    solved = jnp.stack([own(0), own(1)], axis=1)
    return solved, reduced


def solution(mesh):
    devices = Mesh(mesh.devices.reshape(X, C, Z, Y), ("x", "c", "z", "y"))
    placed = (
        P(ROWS, None, COLS),
        P(None, COLS, None),
        P(COLS, None),
        P(None, COLS, ROWS),
        P(COLS, ROWS),
    )
    return jax.shard_map(
        body,
        mesh=devices,
        in_specs=placed,
        out_specs=(P(ROWS, None, COLS), P(COLS, ROWS)),
        check_vma=False,
    )
```

```python
import functools

import jax
import jax.numpy as jnp
from jax import lax
from jax.experimental import pallas as pl
from jax.experimental.pallas import tpu as pltpu
from jax.sharding import Mesh, PartitionSpec as P

X, C, Z, Y = 4, 2, 8, 4
ROWS = ("x", "c")
COLS = ("z", "y")
SPREAD = ("x", "c", "y")
QUAD = 4
NEAR = (0, -1, 1, 2, -2)
VMEM = pl.BlockSpec(memory_space=pltpu.VMEM)
ANY = pl.BlockSpec(memory_space=pl.ANY)
SMEM = pl.BlockSpec(memory_space=pltpu.SMEM)


def f32(*shape):
    return jax.ShapeDtypeStruct(shape, jnp.float32)


def call(kernel, outs, ins, out_specs, in_specs, scratch=(), flops=0, moved=0, limit=16):
    return pl.pallas_call(
        kernel,
        out_shape=outs,
        in_specs=in_specs,
        out_specs=out_specs,
        scratch_shapes=scratch,
        compiler_params=pltpu.CompilerParams(vmem_limit_bytes=limit << 20),
        cost_estimate=pl.CostEstimate(flops=flops, bytes_accessed=moved, transcendentals=0),
    )(*ins)


def exact_dot(left, right):
    return lax.dot_general(
        left, right, (((1,), (0,)), ((), ())),
        precision=lax.Precision.HIGHEST, preferred_element_type=jnp.float32,
    )


def split(value):
    high = value.astype(jnp.bfloat16)
    return high, (value - high.astype(jnp.float32)).astype(jnp.bfloat16)


def copy_all(copies, sems):
    started = [pltpu.make_async_copy(src, dst, sems.at[i]) for i, (src, dst) in enumerate(copies)]
    for copy in started:
        copy.start()
    for copy in started:
        copy.wait()


def open_kernel(rhs, inverse, terms):
    product = exact_dot(rhs[...], inverse[0])
    rows = rhs.shape[0] // Y
    for z in range(Z):
        for y in range(Y):
            terms[z * Y + y] = product[y * rows:(y + 1) * rows, z * 128:(z + 1) * 128]


def share_kernel(place, rhs, inverse, couple, *shared):
    for r in range(Y):
        rows = pl.ds(pl.multiple_of((place[1] + r) % Y * 16, 16), 16)
        piece = rhs[rows]
        shared[r][0:32] = couple[...]
        shared[r][32:64] = inverse[1]
        shared[r][64:72] = jnp.zeros((8, shared[r].shape[1]), jnp.float32)
        shared[r][64:72, 0:128] = piece[0:8]
        shared[r][64:72, 128:256] = piece[8:16]


def in_order(place, shared, rows, matrix):
    for r in range(Y):
        matrix[(place[1] + Y - r) % Y] = shared[r][rows]
    return matrix[...].reshape(Y * 32, -1)


def couple_kernel(place, arrived, *refs):
    shared, (terms, matrix) = refs[:Y], refs[-2:]
    total = jnp.sum(arrived[...], axis=0)
    product = exact_dot(total, in_order(place, shared, slice(0, 32), matrix))
    for z in range(Z):
        terms[z, 0] = product[:, z * 128:(z + 1) * 128]
        terms[z, 1] = total


def latter_kernel(place, arrived, *refs):
    shared, (terms, matrix) = refs[:Y], refs[-2:]
    rhs = sum(piece[64:72] for piece in shared)
    rhs = jnp.concatenate([rhs[:, 0:128], rhs[:, 128:256]], axis=0)
    second = rhs - jnp.sum(arrived[:, 0], axis=0)
    product = exact_dot(second, in_order(place, shared, slice(32, 64), matrix))
    part = lambda z: product[:, (z % Z) * 128:(z % Z + 1) * 128]
    for z in range(Z):
        for k, step in enumerate(NEAR):
            terms[z, k] = part(z + step)


def close_kernel(place, first, arrived, *refs):
    copies = refs[-1]
    latter = jnp.sum(arrived[...], axis=0)
    near = [first[(place[0] + Z + step) % Z, 1] for step in NEAR]
    for target in range(X * C * Y):
        for k in range(QUAD):
            pick = k if k < 3 else 3 + target // Y % C
            copies[target, k] = near[pick]
            copies[target, QUAD + k] = latter[pick]


def around(z):
    return (z % QUAD, (z + 1) % QUAD, (z + 3) % QUAD, (z + 2) % QUAD)


def cut_kernel(place, factor, *refs):
    by_class, by_y, sems = refs[:4], refs[4:8], refs[8]
    classes = around(place[0])
    width = by_y[0].shape[2]
    copies = []
    for r in range(Y):
        for k in range(QUAD):
            strip = pl.multiple_of((classes[k] * Y + (place[1] + r) % Y) * width, width)
            copies.append((factor.at[0, :, pl.ds(strip, width)], by_class[k].at[r]))
            copies.append((factor.at[1, :, pl.ds(strip, width)], by_y[r].at[k]))
    copy_all(copies, sems)


def turn_kernel(*refs):
    arrived, sent, sems = refs[:4], refs[4:8], refs[8]
    copy_all([(arrived[k].at[r], sent[r].at[k]) for r in range(Y) for k in range(QUAD)], sems)


def merge_kernel(place, *refs):
    arrived, sent, sems = refs[:4], refs[4:8], refs[8]
    copy_all([(arrived[r].at[k], sent[k].at[(place[1] + Y - r) % Y]) for r in range(Y) for k in range(QUAD)], sems)


def update_kernel(place, rows, *refs):
    by_r, by_k = refs[:Y], refs[Y:Y + QUAD]
    out, factor, high, low, result, sems = refs[Y + QUAD:]
    start = lambda src, dst, i: pltpu.make_async_copy(src, dst, sems.at[i])
    slots = [(place[1] + Y - r) % Y for r in range(Y)]
    arriving = [start(by_r[r], factor.at[0, r], r) for r in range(Y)]
    arriving += [start(by_k[k], factor.at[1, k], Y + k) for k in range(QUAD)]
    for copy in arriving:
        copy.start()
    left_high, left_low = split(jnp.concatenate([rows[:, k].reshape(-1, 128) for k in range(2 * QUAD)], axis=1))
    for r in range(Y):
        arriving[r].wait()
        high[0, :, slots[r]], low[0, :, slots[r]] = split(factor[0, r])
    for k in range(QUAD):
        arriving[Y + k].wait()
        high[1, k], low[1, k] = split(factor[1, k])
    dot = functools.partial(jnp.dot, preferred_element_type=jnp.float32)
    width = result.shape[2]
    sent = []
    for i, begin in enumerate(range(0, width, 256)):
        at = slice(begin, min(begin + 256, width))
        right_high, right_low = (part[..., at].reshape(2 * QUAD * 128, -1) for part in (high, low))
        product = dot(left_high, right_high) + (dot(left_high, right_low) + dot(left_low, right_high))
        result[..., at] = product.reshape(result.shape[0], 16, -1)
        sent.append(start(result.at[..., at], out.at[..., at], Y + QUAD + i))
        sent[-1].start()
    for copy in sent:
        copy.wait()


def shift_y(value, step):
    return lax.ppermute(value, "y", [(y, (y + step) % Y) for y in range(Y)])


def shift_z(value, step):
    return lax.ppermute(value, "z", [(z, (z + step) % Z) for z in range(Z)])


def shift_far(value):
    pairs = [
        (c * Z + z, c * Z + (z + (2 if c else -2)) % Z) for c in range(C) for z in range(Z)
    ]
    return lax.ppermute(value, ("c", "z"), pairs)


def to_windows(own, up, down, far):
    return own, shift_z(up, 1), shift_z(down, -1), shift_far(far)


def to_ys(own, *others):
    return own, *(shift_y(other, step + 1) for step, other in enumerate(others))


def exchange(value, axes):
    return lax.all_to_all(value, axes, 0, 0, tiled=True)


def body(panel_rhs, diag_inv, coupling, trail_factor, trail_rhs):
    z, y = lax.axis_index("z"), lax.axis_index("y")
    prow = lax.axis_index("x") * C + lax.axis_index("c")
    place = jnp.stack([z, y]).astype(jnp.int32)
    strip, narrow = panel_rhs.shape[0], panel_rhs.shape[2]
    width = trail_rhs.shape[1] // (QUAD * Y)
    block = f32(QUAD, 32, width)
    sems = lambda n: [pltpu.SemaphoreType.DMA((n,))]
    matrix = [pltpu.VMEM((Y, 32, 1024), jnp.float32)]

    rhs = panel_rhs.transpose(1, 0, 2)
    lanes = lax.broadcasted_iota(jnp.int32, (1, 128), 1) // narrow
    second_rhs = jnp.where(lanes == y, jnp.tile(rhs[1], (1, Y)), 0.0)
    terms = call(open_kernel, f32(Z * Y, 16, 128), (rhs[0], diag_inv), VMEM, (VMEM,) * 2)
    arrived = exchange(terms, COLS)
    shared = call(
        share_kernel, (f32(72, 1024),) * Y, (place, second_rhs, diag_inv, coupling),
        (VMEM,) * Y, (SMEM,) + (VMEM,) * 3,
    )
    shared = to_ys(*shared)

    cut = call(
        cut_kernel, (block,) * 8, (place, trail_factor), (ANY,) * 8, (SMEM, VMEM), sems(32), moved=7340032, limit=60,
    )
    by_class, by_y = to_windows(*cut[:4]), to_ys(*cut[4:])

    terms = call(
        couple_kernel, f32(Z, 2, 16, 128), (place, arrived, *shared, cut[0], cut[4]),
        VMEM, (SMEM,) + (VMEM,) * 5 + (ANY,) * 2, matrix, limit=60,
    )
    first = exchange(terms, "z")
    by_r = call(turn_kernel, (block,) * 4, by_class, (ANY,) * 4, (VMEM,) * 4, sems(16), moved=3670016, limit=60)
    first_factor = to_ys(*by_r)

    terms = call(
        latter_kernel, f32(Z, len(NEAR), 16, 128), (place, first, *shared, *by_class[1:], *by_y[1:]),
        VMEM, (SMEM,) + (VMEM,) * 5 + (ANY,) * 6, matrix, limit=60,
    )
    arrived = exchange(terms, "z")
    by_k = call(merge_kernel, (block,) * 4, (place, *by_y), (ANY,) * 4, (SMEM,) + (VMEM,) * 4, sems(16), moved=3670016, limit=60)
    latter_factor = to_windows(*by_k)
    copies = call(close_kernel, f32(X * C * Y, 2 * QUAD, 16, 128), (place, first, arrived, first_factor[1], first_factor[3], by_k[0]), VMEM, (SMEM, VMEM, VMEM) + (ANY,) * 3)
    rows = exchange(copies, SPREAD)

    factor = lambda dtype: pltpu.VMEM((2, QUAD, *block.shape), dtype)
    update = call(
        update_kernel, f32(X * C * Y, 16, width), (place, rows, *first_factor, *latter_factor),
        ANY, (SMEM, VMEM) + (ANY,) * 8,
        [factor(jnp.float32), factor(jnp.bfloat16), factor(jnp.bfloat16), pltpu.VMEM((X * C * Y, 16, width), jnp.float32)] + sems(12),
        flops=2818572288, moved=7602176, limit=56,
    )
    parts = exchange(update, COLS)
    parts = parts.reshape(2, QUAD * Y, *parts.shape[1:])
    reduced = trail_rhs - (parts[0] + parts[1]).transpose(1, 0, 2).reshape(trail_rhs.shape)

    own = lambda panel: lax.dynamic_slice(
        rows, (prow * Y, panel * QUAD, 0, y * narrow), (Y, 1, rows.shape[2], narrow)
    ).reshape(strip, narrow)
    solved = jnp.stack([own(0), own(1)], axis=1)
    return solved, reduced


def solution(mesh):
    devices = Mesh(mesh.devices.reshape(X, C, Z, Y), ("x", "c", "z", "y"))
    placed = (
        P(ROWS, None, COLS),
        P(None, COLS, None),
        P(COLS, None),
        P(None, COLS, ROWS),
        P(COLS, ROWS),
    )
    return jax.shard_map(
        body,
        mesh=devices,
        in_specs=placed,
        out_specs=(P(ROWS, None, COLS), P(COLS, ROWS)),
        check_vma=False,
    )
```

```python
import functools

import jax
import jax.numpy as jnp
from jax import lax
from jax.experimental import pallas as pl
from jax.experimental.pallas import tpu as pltpu
from jax.sharding import Mesh, PartitionSpec as P

X, C, Z, Y = 4, 2, 8, 4
ROWS = ("x", "c")
COLS = ("z", "y")
SPREAD = ("x", "c", "y")
QUAD = 4
NEAR = (0, -1, 1, 2, -2)
VMEM = pl.BlockSpec(memory_space=pltpu.VMEM)
ANY = pl.BlockSpec(memory_space=pl.ANY)
SMEM = pl.BlockSpec(memory_space=pltpu.SMEM)


def f32(*shape):
    return jax.ShapeDtypeStruct(shape, jnp.float32)


def call(kernel, outs, ins, out_specs, in_specs, scratch=(), flops=0, moved=0, limit=16):
    return pl.pallas_call(
        kernel,
        out_shape=outs,
        in_specs=in_specs,
        out_specs=out_specs,
        scratch_shapes=scratch,
        compiler_params=pltpu.CompilerParams(vmem_limit_bytes=limit << 20),
        cost_estimate=pl.CostEstimate(flops=flops, bytes_accessed=moved, transcendentals=0),
    )(*ins)


def exact_dot(left, right):
    return lax.dot_general(
        left, right, (((1,), (0,)), ((), ())),
        precision=lax.Precision.HIGHEST, preferred_element_type=jnp.float32,
    )


def split(value):
    high = value.astype(jnp.bfloat16)
    return high, (value - high.astype(jnp.float32)).astype(jnp.bfloat16)


def copy_all(copies, sems):
    started = [pltpu.make_async_copy(src, dst, sems.at[i]) for i, (src, dst) in enumerate(copies)]
    for copy in started:
        copy.start()
    for copy in started:
        copy.wait()


def open_kernel(rhs, inverse, terms):
    product = exact_dot(rhs[...], inverse[0])
    rows = rhs.shape[0] // Y
    for z in range(Z):
        for y in range(Y):
            terms[z * Y + y] = product[y * rows:(y + 1) * rows, z * 128:(z + 1) * 128]


def share_kernel(place, rhs, inverse, couple, *shared):
    for r in range(Y):
        rows = pl.ds(pl.multiple_of((place[1] + r) % Y * 16, 16), 16)
        piece = rhs[rows]
        shared[r][0:32] = couple[...]
        shared[r][32:64] = inverse[1]
        shared[r][64:72] = jnp.zeros((8, shared[r].shape[1]), jnp.float32)
        shared[r][64:72, 0:128] = piece[0:8]
        shared[r][64:72, 128:256] = piece[8:16]


def fetch(place, shared, rows, matrix, sems):
    copies = [
        pltpu.make_async_copy(shared[r].at[rows], matrix.at[(place[1] + Y - r) % Y], sems.at[r]) for r in range(Y)
    ]
    for copy in copies:
        copy.start()
    return copies


def couple_kernel(place, arrived, *refs):
    shared, (terms, matrix, sems) = refs[:Y], refs[-3:]
    copies = fetch(place, shared, pl.ds(0, 32), matrix, sems)
    total = jnp.sum(arrived[...], axis=0)
    for copy in copies:
        copy.wait()
    product = exact_dot(total, matrix[...].reshape(Y * 32, -1))
    for z in range(Z):
        terms[z, 0] = product[:, z * 128:(z + 1) * 128]
        terms[z, 1] = total


def latter_kernel(place, arrived, *refs):
    shared, (terms, matrix, sems) = refs[:Y], refs[-3:]
    copies = fetch(place, shared, pl.ds(32, 40), matrix, sems)
    for copy in copies:
        copy.wait()
    rhs = jnp.sum(matrix[:, 32:40], axis=0)
    rhs = jnp.concatenate([rhs[:, 0:128], rhs[:, 128:256]], axis=0)
    second = rhs - jnp.sum(arrived[:, 0], axis=0)
    product = exact_dot(second, matrix[:, 0:32].reshape(Y * 32, -1))
    part = lambda z: product[:, (z % Z) * 128:(z % Z + 1) * 128]
    for z in range(Z):
        for k, step in enumerate(NEAR):
            terms[z, k] = part(z + step)


def close_kernel(place, first, arrived, *refs):
    copies = refs[-1]
    latter = jnp.sum(arrived[...], axis=0)
    near = [first[(place[0] + Z + step) % Z, 1] for step in NEAR]
    for target in range(X * C * Y):
        for k in range(QUAD):
            pick = k if k < 3 else 3 + target // Y % C
            copies[target, k] = near[pick]
            copies[target, QUAD + k] = latter[pick]


def around(z):
    return (z % QUAD, (z + 1) % QUAD, (z + 3) % QUAD, (z + 2) % QUAD)


def cut_kernel(place, factor, *refs):
    by_class, by_y, sems = refs[:4], refs[4:8], refs[8]
    classes = around(place[0])
    width = by_y[0].shape[2]
    copies = []
    for r in range(Y):
        for k in range(QUAD):
            strip = pl.multiple_of((classes[k] * Y + (place[1] + r) % Y) * width, width)
            copies.append((factor.at[0, :, pl.ds(strip, width)], by_class[k].at[r]))
            copies.append((factor.at[1, :, pl.ds(strip, width)], by_y[r].at[k]))
    copy_all(copies, sems)


def turn_kernel(*refs):
    arrived, sent, sems = refs[:4], refs[4:8], refs[8]
    copy_all([(arrived[k].at[r], sent[r].at[k]) for r in range(Y) for k in range(QUAD)], sems)


def merge_kernel(place, *refs):
    arrived, sent, sems = refs[:4], refs[4:8], refs[8]
    copy_all([(arrived[r].at[k], sent[k].at[(place[1] + Y - r) % Y]) for r in range(Y) for k in range(QUAD)], sems)


def update_kernel(place, rows, *refs):
    by_r, by_k = refs[:Y], refs[Y:Y + QUAD]
    out, factor, high, low, result, sems = refs[Y + QUAD:]
    start = lambda src, dst, i: pltpu.make_async_copy(src, dst, sems.at[i])
    slots = [(place[1] + Y - r) % Y for r in range(Y)]
    arriving = [start(by_r[r], factor.at[0, r], r) for r in range(Y)]
    arriving += [start(by_k[k], factor.at[1, k], Y + k) for k in range(QUAD)]
    for copy in arriving:
        copy.start()
    left_high, left_low = split(jnp.concatenate([rows[:, k].reshape(-1, 128) for k in range(2 * QUAD)], axis=1))
    for r in range(Y):
        arriving[r].wait()
        high[0, :, slots[r]], low[0, :, slots[r]] = split(factor[0, r])
    for k in range(QUAD):
        arriving[Y + k].wait()
        high[1, k], low[1, k] = split(factor[1, k])
    dot = functools.partial(jnp.dot, preferred_element_type=jnp.float32)
    width = result.shape[2]
    sent = []
    for i, begin in enumerate(range(0, width, 256)):
        at = slice(begin, min(begin + 256, width))
        right_high, right_low = (part[..., at].reshape(2 * QUAD * 128, -1) for part in (high, low))
        product = dot(left_high, right_high) + (dot(left_high, right_low) + dot(left_low, right_high))
        result[..., at] = product.reshape(result.shape[0], 16, -1)
        sent.append(start(result.at[..., at], out.at[..., at], Y + QUAD + i))
        sent[-1].start()
    for copy in sent:
        copy.wait()


def shift_y(value, step):
    return lax.ppermute(value, "y", [(y, (y + step) % Y) for y in range(Y)])


def shift_z(value, step):
    return lax.ppermute(value, "z", [(z, (z + step) % Z) for z in range(Z)])


def shift_far(value):
    pairs = [
        (c * Z + z, c * Z + (z + (2 if c else -2)) % Z) for c in range(C) for z in range(Z)
    ]
    return lax.ppermute(value, ("c", "z"), pairs)


def to_windows(own, up, down, far):
    return own, shift_z(up, 1), shift_z(down, -1), shift_far(far)


def to_ys(own, *others):
    return own, *(shift_y(other, step + 1) for step, other in enumerate(others))


def exchange(value, axes):
    return lax.all_to_all(value, axes, 0, 0, tiled=True)


def body(panel_rhs, diag_inv, coupling, trail_factor, trail_rhs):
    z, y = lax.axis_index("z"), lax.axis_index("y")
    prow = lax.axis_index("x") * C + lax.axis_index("c")
    place = jnp.stack([z, y]).astype(jnp.int32)
    strip, narrow = panel_rhs.shape[0], panel_rhs.shape[2]
    width = trail_rhs.shape[1] // (QUAD * Y)
    block = f32(QUAD, 32, width)
    sems = lambda n: [pltpu.SemaphoreType.DMA((n,))]
    matrix = lambda rows: [pltpu.VMEM((Y, rows, 1024), jnp.float32)] + sems(Y)

    rhs = panel_rhs.transpose(1, 0, 2)
    lanes = lax.broadcasted_iota(jnp.int32, (1, 128), 1) // narrow
    second_rhs = jnp.where(lanes == y, jnp.tile(rhs[1], (1, Y)), 0.0)
    terms = call(open_kernel, f32(Z * Y, 16, 128), (rhs[0], diag_inv), VMEM, (VMEM,) * 2)
    arrived = exchange(terms, COLS)
    shared = call(
        share_kernel, (f32(72, 1024),) * Y, (place, second_rhs, diag_inv, coupling),
        (VMEM,) * Y, (SMEM,) + (VMEM,) * 3,
    )
    shared = to_ys(*shared)

    cut = call(
        cut_kernel, (block,) * 8, (place, trail_factor), (ANY,) * 8, (SMEM, VMEM), sems(32), moved=7340032, limit=60,
    )
    by_class, by_y = to_windows(*cut[:4]), to_ys(*cut[4:])

    terms = call(
        couple_kernel, f32(Z, 2, 16, 128), (place, arrived, *shared, cut[0], cut[4]),
        VMEM, (SMEM, VMEM) + (ANY,) * 6, matrix(32), limit=60,
    )
    first = exchange(terms, "z")
    by_r = call(turn_kernel, (block,) * 4, by_class, (ANY,) * 4, (VMEM,) * 4, sems(16), moved=3670016, limit=60)
    first_factor = to_ys(*by_r)

    terms = call(
        latter_kernel, f32(Z, len(NEAR), 16, 128), (place, first, *shared, *by_class[1:], *by_y[1:]),
        VMEM, (SMEM, VMEM) + (ANY,) * 10, matrix(40), limit=60,
    )
    arrived = exchange(terms, "z")
    by_k = call(merge_kernel, (block,) * 4, (place, *by_y), (ANY,) * 4, (SMEM,) + (VMEM,) * 4, sems(16), moved=3670016, limit=60)
    latter_factor = to_windows(*by_k)
    copies = call(close_kernel, f32(X * C * Y, 2 * QUAD, 16, 128), (place, first, arrived, first_factor[1], first_factor[3]), VMEM, (SMEM, VMEM, VMEM, ANY, ANY))
    rows = exchange(copies, SPREAD)

    factor = lambda dtype: pltpu.VMEM((2, QUAD, *block.shape), dtype)
    update = call(
        update_kernel, f32(X * C * Y, 16, width), (place, rows, *first_factor, *latter_factor),
        ANY, (SMEM, VMEM) + (ANY,) * 8,
        [factor(jnp.float32), factor(jnp.bfloat16), factor(jnp.bfloat16), pltpu.VMEM((X * C * Y, 16, width), jnp.float32)] + sems(12),
        flops=2818572288, moved=7602176, limit=56,
    )
    parts = exchange(update, COLS)
    parts = parts.reshape(2, QUAD * Y, *parts.shape[1:])
    reduced = trail_rhs - (parts[0] + parts[1]).transpose(1, 0, 2).reshape(trail_rhs.shape)

    own = lambda panel: lax.dynamic_slice(
        rows, (prow * Y, panel * QUAD, 0, y * narrow), (Y, 1, rows.shape[2], narrow)
    ).reshape(strip, narrow)
    solved = jnp.stack([own(0), own(1)], axis=1)
    return solved, reduced


def solution(mesh):
    devices = Mesh(mesh.devices.reshape(X, C, Z, Y), ("x", "c", "z", "y"))
    placed = (
        P(ROWS, None, COLS),
        P(None, COLS, None),
        P(COLS, None),
        P(None, COLS, ROWS),
        P(COLS, ROWS),
    )
    return jax.shard_map(
        body,
        mesh=devices,
        in_specs=placed,
        out_specs=(P(ROWS, None, COLS), P(COLS, ROWS)),
        check_vma=False,
    )
```
